1024 devices in a mesh: comp: 16 (over z, core), lat: 64 (over y, x).
Axes of the slice: x: 8, y: 8, z: 8, core: 2. Of those that a mesh axis runs over, the one named last changes fastest.
Arguments:
- spectrum: float32 [1152, 128, 2048], P('comp', 'lat'), may hold values from 0.1 to 2
- courant_lat: float32 [1152], P('comp'), may hold values from -0.45 to 0.45
- courant_lon: float32 [1152], P('comp'), may hold values from -0.45 to 0.45
- sea_mask: int32 [128, 2048], P('lat'), may hold values from 0 to 1, as said below
- strength: float32 [1152], replicated, may hold values from 0.02 to 0.2
- quad_shift: int32 [4, 2], replicated, may hold values from -4 to 4
Outputs:
- spectrum_next: float32 [1152, 128, 2048], P('comp', 'lat')
The draws below stay inside these ranges and needn't reach their ends.
Inputs may be any that keep to these rules, and one draw needn't show every extreme that they name: `quad_shift`: column 0 offsets frequency, column 1 offsets direction. `sea_mask`: each aligned block of 2 rows holds at most 3072 sea points, and some block holds exactly 3072.
All inputs are finite; a program needn't handle non-finite values.
Results may differ from the reference program's by a relative error of at most 0.00002.
Values sent between devices are 32-bit elements; how exact they have to be, the bound alone decides.
A program may use at most 32 MiB of HBM per device.

```python
import math
import jax
import jax.numpy as jnp
from jax import lax

NF = 36
ND = 32
NQ = 4
LAT_DEV = 2
LON = 2048
NC = 1152
LAT = 128


def draw_sea_mask(key, part):
    blocks = LAT // LAT_DEV
    points = LAT_DEV * LON
    most = 3 * points // 4
    key_counts = jax.random.fold_in(key, 11)
    key_top = jax.random.fold_in(key, 12)
    key_place = jax.random.fold_in(key, 13)
    counts = jax.random.randint(key_counts, (blocks,), most // 2, most + 1)
    top_block = jax.random.randint(key_top, (), 0, blocks)
    counts = jnp.where(jnp.arange(blocks) == top_block, most, counts)
    block_keys = jax.random.split(key_place, blocks)
    ranks = jax.vmap(lambda one: jax.random.permutation(one, points))(block_keys)
    marks = (ranks < counts[:, None]).astype(jnp.int32)
    return marks.reshape(LAT, LON)


def with_ends(array, stream_key, low, largest):
    spot = [jax.random.randint(jax.random.fold_in(stream_key, axis), (), 0, length) for axis, length in enumerate(array.shape)]
    main_axis = array.shape.index(max(array.shape))
    neighbour = spot[:main_axis] + [(spot[main_axis] + 1) % array.shape[main_axis]] + spot[main_axis + 1:]
    return array.at[tuple(spot)].set(low).at[tuple(neighbour)].set(largest)


def shard_levels(own_key, shape, cuts, smallest, largest):
    def one(position, blocks):
        draws = jax.random.uniform(jax.random.fold_in(jax.random.fold_in(own_key, 6), position), (blocks,), jnp.float32, smallest / len(cuts), largest / len(cuts))
        return jnp.repeat(jnp.exp(draws), shape[position] // blocks).reshape((-1,) + (1,) * (len(shape) - position - 1))

    loudness = one(*cuts[0])
    for cut in cuts[1:]:
        loudness = loudness * one(*cut)
    return loudness


def setup_inputs(seed: int = 0) -> dict:
    keys = jax.random.split(jax.random.key(seed), 7)
    spectrum = jnp.clip(0.1 + 1.9 * jax.random.uniform(keys[0], (NC, LAT, LON), jnp.float32) ** shard_levels(keys[0], (NC, LAT, LON), ((0, 16), (1, 64)), -0.2, 0.2), 0.1, 2.0)
    courant_lat = jnp.clip(jax.random.uniform(keys[1], (NC,), jnp.float32, -0.45, 0.45) * shard_levels(keys[1], (NC,), ((0, 16),), -0.4, 0.0), -0.45, 0.45)
    courant_lon = jnp.clip(jax.random.uniform(keys[2], (NC,), jnp.float32, -0.45, 0.45) * shard_levels(keys[2], (NC,), ((0, 16),), -0.4, 0.0), -0.45, 0.45)
    sea_mask = draw_sea_mask(jax.random.fold_in(keys[6], 71), 0)
    strength = jnp.clip(jnp.exp(jax.random.uniform(keys[4], (NC,), jnp.float32, math.log(0.02), math.log(0.2))), 0.02, 0.2)
    quad_shift = with_ends(jax.random.randint(keys[5], (NQ, 2), -4, 5), jax.random.fold_in(keys[5], 1), -4, 4).astype(jnp.int32)
    return {"spectrum": spectrum, "courant_lat": courant_lat, "courant_lon": courant_lon, "sea_mask": sea_mask, "strength": strength, "quad_shift": quad_shift}


reach = 4


def upwind(field, along_lat, along_lon, maskf):
    padded = jnp.pad(field, ((0, 0), (1, 1), (0, 0)))
    south = padded[:, :-2, :]
    north = padded[:, 2:, :]
    west = jnp.roll(field, 1, axis=2)
    east = jnp.roll(field, -1, axis=2)
    plus_a = jnp.maximum(along_lat, 0.0)
    minus_a = jnp.minimum(along_lat, 0.0)
    plus_b = jnp.maximum(along_lon, 0.0)
    minus_b = jnp.minimum(along_lon, 0.0)
    moved = field - plus_a * (field - south) - minus_a * (north - field)
    moved = moved - plus_b * (field - west) - minus_b * (east - field)
    return moved * maskf


def interact(energy, strength, quad_shift):
    rest = energy.shape[1:]
    grid = energy.reshape((NF, ND) + rest)
    widths = ((reach, reach),) + ((0, 0),) * (grid.ndim - 1)
    padded = jnp.pad(grid, widths)
    total = jnp.zeros(grid.shape, jnp.float32)
    for index in range(NQ):
        offset_f = quad_shift[index, 0].astype(jnp.int32)
        offset_d = quad_shift[index, 1].astype(jnp.int32)
        partner = lax.dynamic_slice_in_dim(padded, reach + offset_f, NF, 0)
        partner = jnp.roll(partner, -offset_d, axis=1)
        total = total + partner * (partner - grid)
    coeff = strength.reshape((NF, ND) + (1,) * len(rest))
    return (coeff * grid * total).reshape(energy.shape)


def reference(spectrum, courant_lat, courant_lon, sea_mask, strength, quad_shift):
    maskf = sea_mask.astype(jnp.float32)[None]
    along_lat = courant_lat[:, None, None]
    along_lon = courant_lon[:, None, None]
    field = upwind(spectrum, along_lat, along_lon, maskf)
    field = upwind(field, along_lat, along_lon, maskf)
    rows = jnp.transpose(field, (1, 0, 2))
    updated = lax.map(lambda row: row + interact(row, strength, quad_shift), rows)
    return jnp.transpose(updated, (1, 0, 2))
```

```python
import functools

import jax
import jax.numpy as jnp
from jax import lax
from jax.experimental import pallas as pl
from jax.experimental.pallas import tpu as pltpu
from jax.sharding import PartitionSpec as P

NF = 36
ND = 32
NQ = 4
COMP = 72
CHIP = 2 * COMP
CHUNKS = 9
STEP = COMP // CHUNKS
PIECES = 3
PART = COMP // PIECES

MESH = pl.DeviceIdType.MESH


def roll_lon(e, edge_west, edge_east, low_sub, high_sub):
    down = pltpu.roll(e, 2, axis=1)
    down = jnp.where(low_sub, jnp.concatenate([down[3:], down[:3]], axis=0), down)
    west = pltpu.roll(jnp.where(edge_west, down, e), 1, axis=2)
    up = pltpu.roll(e, 6, axis=1)
    up = jnp.where(high_sub, jnp.concatenate([up[1:], up[:1]], axis=0), up)
    east = pltpu.roll(jnp.where(edge_east, up, e), 127, axis=2)
    return west, east


def kernel(
    n_comp,
    n_lat,
    x_ref,
    lat_ref,
    lon_ref,
    mask_ref,
    strength_ref,
    shift_ref,
    out_ref,
    xv,
    south,
    north,
    mask_south,
    mask_north,
    g,
    other,
    res_own,
    res_sib,
    load_sem,
    x_send,
    x_recv,
    m_send,
    m_recv,
    z_send,
    z_recv,
    swap_send,
    swap_recv,
    ret_send,
    ret_recv,
    out_sem,
):
    comp = lax.axis_index("comp")
    lat = lax.axis_index("lat")
    z = comp // 2
    core = comp % 2
    n_z = n_comp // 2
    has_south = lat > 0
    has_north = lat < n_lat - 1
    has_below = z > 0
    has_above = z < n_z - 1
    sib = z * 2 + 1 - core

    def rows(ch):
        return pl.ds(ch * STEP, STEP)

    def load(ch):
        return pltpu.make_async_copy(x_ref.at[rows(ch)], xv.at[rows(ch)], load_sem.at[ch])

    def to_north(ch):
        return pltpu.make_async_remote_copy(
            src_ref=x_ref.at[rows(ch)],
            dst_ref=south.at[rows(ch)],
            send_sem=x_send.at[0, ch],
            recv_sem=x_recv.at[0, ch],
            device_id={"lat": lat + 1},
            device_id_type=MESH,
        )

    def to_south(ch):
        return pltpu.make_async_remote_copy(
            src_ref=x_ref.at[rows(ch)],
            dst_ref=north.at[rows(ch)],
            send_sem=x_send.at[1, ch],
            recv_sem=x_recv.at[1, ch],
            device_id={"lat": lat - 1},
            device_id_type=MESH,
        )

    def mask_to_north():
        return pltpu.make_async_remote_copy(
            src_ref=mask_ref,
            dst_ref=mask_south,
            send_sem=m_send.at[0],
            recv_sem=m_recv.at[0],
            device_id={"lat": lat + 1},
            device_id_type=MESH,
        )

    def mask_to_south():
        return pltpu.make_async_remote_copy(
            src_ref=mask_ref,
            dst_ref=mask_north,
            send_sem=m_send.at[1],
            recv_sem=m_recv.at[1],
            device_id={"lat": lat - 1},
            device_id_type=MESH,
        )

    def half_src(h, ch):
        if h == 0:
            return g.at[pl.ds(CHIP + core * COMP + ch * STEP, STEP)]
        return other.at[rows(ch)]

    def to_z(direction, h, ch):
        third = 0 if direction == 0 else 2
        target = (z + 1 if direction == 0 else z - 1) * 2 + (core if h == 0 else 1 - core)
        return pltpu.make_async_remote_copy(
            src_ref=half_src(h, ch),
            dst_ref=g.at[pl.ds(third * CHIP + core * COMP + ch * STEP, STEP)],
            send_sem=z_send.at[direction, h, ch],
            recv_sem=z_recv.at[direction, core, ch],
            device_id={"comp": target},
            device_id_type=MESH,
        )

    def from_z(direction, source_core, ch):
        third = 0 if direction == 0 else 2
        here = g.at[pl.ds(third * CHIP + source_core * COMP + ch * STEP, STEP)]
        return pltpu.make_async_remote_copy(
            src_ref=here,
            dst_ref=here,
            send_sem=z_send.at[direction, 0, ch],
            recv_sem=z_recv.at[direction, source_core, ch],
            device_id={"comp": sib},
            device_id_type=MESH,
        )

    def swap(ch):
        return pltpu.make_async_remote_copy(
            src_ref=other.at[rows(ch)],
            dst_ref=g.at[pl.ds(CHIP + core * COMP + ch * STEP, STEP)],
            send_sem=swap_send.at[ch],
            recv_sem=swap_recv.at[ch],
            device_id={"comp": sib},
            device_id_type=MESH,
        )

    def swap_in(ch):
        here = g.at[pl.ds(CHIP + (1 - core) * COMP + ch * STEP, STEP)]
        return pltpu.make_async_remote_copy(
            src_ref=here,
            dst_ref=here,
            send_sem=swap_send.at[ch],
            recv_sem=swap_recv.at[ch],
            device_id={"comp": sib},
            device_id_type=MESH,
        )

    def give_back(piece):
        span = pl.ds(piece * PART, PART)
        return pltpu.make_async_remote_copy(
            src_ref=res_sib.at[span],
            dst_ref=out_ref.at[span, pl.ds(2 * core, 2)],
            send_sem=ret_send.at[piece],
            recv_sem=ret_recv.at[piece],
            device_id={"comp": sib},
            device_id_type=MESH,
        )

    def take_back(piece):
        span = pl.ds(piece * PART, PART)
        return pltpu.make_async_remote_copy(
            src_ref=res_sib.at[span],
            dst_ref=out_ref.at[span, pl.ds(2 * (1 - core), 2)],
            send_sem=ret_send.at[piece],
            recv_sem=ret_recv.at[piece],
            device_id={"comp": sib},
            device_id_type=MESH,
        )

    def write_own(piece):
        span = pl.ds(piece * PART, PART)
        return pltpu.make_async_copy(res_own.at[span], out_ref.at[span, pl.ds(2 * core, 2)], out_sem.at[piece])

    for ch in range(CHUNKS):
        load(ch).start()

    barrier = pltpu.get_barrier_semaphore()

    def greet(**where):
        pl.semaphore_signal(barrier, inc=1, device_id=where, device_id_type=MESH)

    greet(comp=sib)

    @pl.when(has_south)
    def _():
        greet(lat=lat - 1)

    @pl.when(has_north)
    def _():
        greet(lat=lat + 1)

    @pl.when(has_below)
    def _():
        greet(comp=2 * z - 2)
        greet(comp=2 * z - 1)

    @pl.when(has_above)
    def _():
        greet(comp=2 * z + 2)
        greet(comp=2 * z + 3)

    @pl.when(jnp.logical_not(has_south))
    def _():
        south[...] = jnp.zeros_like(south)
        mask_south[...] = jnp.zeros_like(mask_south)

    @pl.when(jnp.logical_not(has_north))
    def _():
        north[...] = jnp.zeros_like(north)
        mask_north[...] = jnp.zeros_like(mask_north)

    @pl.when(jnp.logical_not(has_below))
    def _():
        g[pl.ds(0, CHIP)] = jnp.zeros((CHIP, 2, 8, 128), jnp.float32)

    @pl.when(jnp.logical_not(has_above))
    def _():
        g[pl.ds(2 * CHIP, CHIP)] = jnp.zeros((CHIP, 2, 8, 128), jnp.float32)

    def one(flag):
        return flag.astype(jnp.int32)

    pl.semaphore_wait(barrier, 1 + one(has_south) + one(has_north) + 2 * (one(has_below) + one(has_above)))

    @pl.when(has_north)
    def _():
        mask_to_north().start()

    @pl.when(has_south)
    def _():
        mask_to_south().start()

    for ch in range(CHUNKS):

        @pl.when(has_north)
        def _():
            to_north(ch).start()

        @pl.when(has_south)
        def _():
            to_south(ch).start()

    @pl.when(has_south)
    def _():
        mask_to_north().wait_recv()

    @pl.when(has_north)
    def _():
        mask_to_south().wait_recv()

    shape = (4, 8, 128)
    lane = lax.broadcasted_iota(jnp.int32, shape, 2)
    sub = lax.broadcasted_iota(jnp.int32, shape, 1)
    edge_west = lane == 127
    edge_east = lane == 0
    low_sub = sub < 2
    high_sub = sub >= 6
    odd = (sub & 1) == 1

    def other_row(e):
        return jnp.where(odd, pltpu.roll(e, 1, axis=1), pltpu.roll(e, 7, axis=1))

    mask = mask_ref[...]
    for ch in range(CHUNKS):
        load(ch).wait()

        @pl.when(has_south)
        def _():
            to_north(ch).wait_recv()

        @pl.when(has_north)
        def _():
            to_south(ch).wait_recv()

        def propagate(i, carry):
            a = lat_ref[i]
            b = lon_ref[i]
            up = a > 0.0
            west_in = b > 0.0
            a = jnp.abs(a)
            b = jnp.abs(b)
            from_halo = odd == up

            def substep(e, upstream, m):
                west, east = roll_lon(e, edge_west, edge_east, low_sub, high_sub)
                side = jnp.where(west_in, west, east)
                moved = e - a * (e - upstream)
                moved = moved - b * (e - side)
                return moved * m

            e = xv[i]
            halo = jnp.where(up, south[i], north[i])
            halo_mask = jnp.where(up, mask_south[...], mask_north[...])
            first = substep(e, other_row(jnp.where(from_halo, halo, e)), mask)
            halo = substep(halo, other_row(halo), halo_mask)
            second = substep(first, other_row(jnp.where(from_halo, halo, first)), mask)
            mine = core == 0
            g[CHIP + core * COMP + i] = jnp.where(mine, second[:2], second[2:])
            other[i] = jnp.where(mine, second[2:], second[:2])
            return carry

        lax.fori_loop(ch * STEP, (ch + 1) * STEP, propagate, 0)

        for h in range(2):

            @pl.when(has_above)
            def _():
                to_z(0, h, ch).start()

            @pl.when(has_below)
            def _():
                to_z(1, h, ch).start()

        swap(ch).start()

    for ch in range(CHUNKS):
        swap_in(ch).wait_recv()
        for source_core in range(2):

            @pl.when(has_below)
            def _():
                from_z(0, source_core, ch).wait_recv()

            @pl.when(has_above)
            def _():
                from_z(1, source_core, ch).wait_recv()

    base = z * CHIP

    def source(i):
        k = base + i
        d = k & (ND - 1)
        e = g[CHIP + i]
        total = jnp.zeros_like(e)
        for q in range(NQ):
            place = CHIP + i - d + ND * shift_ref[q, 0] + ((d + shift_ref[q, 1]) & (ND - 1))
            partner = g[place]
            total = total + partner * (partner - e)
        return e + (strength_ref[k] * e) * total

    for piece in range(PIECES):

        def for_sibling(i, carry):
            res_sib[i] = source((1 - core) * COMP + i)
            return carry

        lax.fori_loop(piece * PART, (piece + 1) * PART, for_sibling, 0)
        give_back(piece).start()

    for piece in range(PIECES):

        def for_me(i, carry):
            res_own[i] = source(core * COMP + i)
            return carry

        lax.fori_loop(piece * PART, (piece + 1) * PART, for_me, 0)
        write_own(piece).start()

    for ch in range(CHUNKS):

        @pl.when(has_north)
        def _():
            to_north(ch).wait_send()

        @pl.when(has_south)
        def _():
            to_south(ch).wait_send()

        for h in range(2):

            @pl.when(has_above)
            def _():
                to_z(0, h, ch).wait_send()

            @pl.when(has_below)
            def _():
                to_z(1, h, ch).wait_send()

        swap(ch).wait_send()

    @pl.when(has_north)
    def _():
        mask_to_north().wait_send()

    @pl.when(has_south)
    def _():
        mask_to_south().wait_send()

    for piece in range(PIECES):
        give_back(piece).wait_send()
        take_back(piece).wait_recv()
        write_own(piece).wait()


def solution(mesh):
    n_comp, n_lat = mesh.shape["comp"], mesh.shape["lat"]
    block = pltpu.VMEM((COMP, 4, 8, 128), jnp.float32)
    half = pltpu.VMEM((COMP, 2, 8, 128), jnp.float32)
    small = pltpu.VMEM((4, 8, 128), jnp.float32)
    dma = pltpu.SemaphoreType.DMA

    def per_device(spectrum, courant_lat, courant_lon, sea_mask, strength, quad_shift):
        x = spectrum.reshape(COMP, 2, 16, 128).transpose(0, 2, 1, 3).reshape(COMP, 4, 8, 128)
        mask = sea_mask.astype(jnp.float32).reshape(2, 16, 128).transpose(1, 0, 2).reshape(4, 8, 128)
        smem = pl.BlockSpec(memory_space=pltpu.SMEM)
        out = pl.pallas_call(
            functools.partial(kernel, n_comp, n_lat),
            out_shape=jax.ShapeDtypeStruct((COMP, 4, 8, 128), jnp.float32),
            in_specs=[
                pl.BlockSpec(memory_space=pl.ANY),
                smem,
                smem,
                pl.BlockSpec(memory_space=pltpu.VMEM),
                smem,
                smem,
            ],
            out_specs=pl.BlockSpec(memory_space=pl.ANY),
            scratch_shapes=[
                block,
                block,
                block,
                small,
                small,
                pltpu.VMEM((3 * CHIP, 2, 8, 128), jnp.float32),
                half,
                half,
                half,
                dma((CHUNKS,)),
                dma((2, CHUNKS)),
                dma((2, CHUNKS)),
                dma((2,)),
                dma((2,)),
                dma((2, 2, CHUNKS)),
                dma((2, 2, CHUNKS)),
                dma((CHUNKS,)),
                dma((CHUNKS,)),
                dma((PIECES,)),
                dma((PIECES,)),
                dma((PIECES,)),
            ],
            compiler_params=pltpu.CompilerParams(
                collective_id=0, has_side_effects=True, vmem_limit_bytes=40 * 1024 * 1024
            ),
        )(x, courant_lat, courant_lon, mask, strength, quad_shift)
        return out.reshape(COMP, 16, 2, 128).transpose(0, 2, 1, 3).reshape(COMP, 2, 2048)

    return jax.shard_map(
        per_device,
        mesh=mesh,
        in_specs=(P("comp", "lat", None), P("comp"), P("comp"), P("lat", None), P(), P()),
        out_specs=P("comp", "lat", None),
        check_vma=False,
    )
```

```python
import functools

import jax
import jax.numpy as jnp
from jax import lax
from jax.experimental import pallas as pl
from jax.experimental.pallas import tpu as pltpu
from jax.sharding import PartitionSpec as P

NF = 36
ND = 32
NQ = 4
COMP = 72
CHIP = 2 * COMP
CHUNKS = 9
STEP = COMP // CHUNKS
PIECES = 3
PART = COMP // PIECES
VMEM_BYTES = 627 * 1024 * 1024 // 10
ROW = 8
FAR = (ROW + 1, 2 * ROW + 1, 3 * ROW + 1)

MESH = pl.DeviceIdType.MESH


def roll_lon(e, edge_west, edge_east, low_sub, high_sub):
    down = pltpu.roll(e, 2, axis=1)
    down = jnp.where(low_sub, jnp.concatenate([down[3:], down[:3]], axis=0), down)
    west = pltpu.roll(jnp.where(edge_west, down, e), 1, axis=2)
    up = pltpu.roll(e, 6, axis=1)
    up = jnp.where(high_sub, jnp.concatenate([up[1:], up[:1]], axis=0), up)
    east = pltpu.roll(jnp.where(edge_east, up, e), 127, axis=2)
    return west, east


def kernel(
    n_comp,
    n_lat,
    x_ref,
    lat_any,
    lon_any,
    mask_any,
    strength_any,
    shift_any,
    out_ref,
    lat_ref,
    lon_ref,
    strength_ref,
    shift_ref,
    place_ref,
    mask_ref,
    xv,
    south,
    north,
    mask_south,
    mask_north,
    g,
    other,
    res_sib,
    arg_sem,
    load_sem,
    x_send,
    x_recv,
    m_send,
    m_recv,
    z_send,
    z_recv,
    swap_send,
    swap_recv,
    ret_send,
    ret_recv,
):
    comp = lax.axis_index("comp")
    lat = lax.axis_index("lat")
    z = comp // 2
    core = comp % 2
    n_z = n_comp // 2
    has_south = lat > 0
    has_north = lat < n_lat - 1
    has_below = z > 0
    has_above = z < n_z - 1
    sib = z * 2 + 1 - core

    def rows(ch):
        return pl.ds(ch * STEP, STEP)

    def load(ch):
        return pltpu.make_async_copy(x_ref.at[rows(ch)], xv.at[rows(ch)], load_sem.at[ch])

    def to_north(ch):
        return pltpu.make_async_remote_copy(
            src_ref=x_ref.at[rows(ch)],
            dst_ref=south.at[rows(ch)],
            send_sem=x_send.at[0, ch],
            recv_sem=x_recv.at[0, ch],
            device_id={"lat": lat + 1},
            device_id_type=MESH,
        )

    def to_south(ch):
        return pltpu.make_async_remote_copy(
            src_ref=x_ref.at[rows(ch)],
            dst_ref=north.at[rows(ch)],
            send_sem=x_send.at[1, ch],
            recv_sem=x_recv.at[1, ch],
            device_id={"lat": lat - 1},
            device_id_type=MESH,
        )

    def mask_to_north():
        return pltpu.make_async_remote_copy(
            src_ref=mask_any,
            dst_ref=mask_south,
            send_sem=m_send.at[0],
            recv_sem=m_recv.at[0],
            device_id={"lat": lat + 1},
            device_id_type=MESH,
        )

    def mask_to_south():
        return pltpu.make_async_remote_copy(
            src_ref=mask_any,
            dst_ref=mask_north,
            send_sem=m_send.at[1],
            recv_sem=m_recv.at[1],
            device_id={"lat": lat - 1},
            device_id_type=MESH,
        )

    def half_src(h, ch):
        if h == 0:
            return g.at[pl.ds(CHIP + core * COMP + ch * STEP, STEP)]
        return other.at[rows(ch)]

    def to_z(direction, h, ch):
        third = 0 if direction == 0 else 2
        target = (z + 1 if direction == 0 else z - 1) * 2 + (core if h == 0 else 1 - core)
        return pltpu.make_async_remote_copy(
            src_ref=half_src(h, ch),
            dst_ref=g.at[pl.ds(third * CHIP + core * COMP + ch * STEP, STEP)],
            send_sem=z_send.at[direction, h, ch],
            recv_sem=z_recv.at[direction, core, ch],
            device_id={"comp": target},
            device_id_type=MESH,
        )

    def from_z(direction, source_core, ch):
        third = 0 if direction == 0 else 2
        here = g.at[pl.ds(third * CHIP + source_core * COMP + ch * STEP, STEP)]
        return pltpu.make_async_remote_copy(
            src_ref=here,
            dst_ref=here,
            send_sem=z_send.at[direction, 0, ch],
            recv_sem=z_recv.at[direction, source_core, ch],
            device_id={"comp": sib},
            device_id_type=MESH,
        )

    def swap(ch):
        return pltpu.make_async_remote_copy(
            src_ref=other.at[rows(ch)],
            dst_ref=g.at[pl.ds(CHIP + core * COMP + ch * STEP, STEP)],
            send_sem=swap_send.at[ch],
            recv_sem=swap_recv.at[ch],
            device_id={"comp": sib},
            device_id_type=MESH,
        )

    def swap_in(ch):
        here = g.at[pl.ds(CHIP + (1 - core) * COMP + ch * STEP, STEP)]
        return pltpu.make_async_remote_copy(
            src_ref=here,
            dst_ref=here,
            send_sem=swap_send.at[ch],
            recv_sem=swap_recv.at[ch],
            device_id={"comp": sib},
            device_id_type=MESH,
        )

    def give_back(piece):
        span = pl.ds(piece * PART, PART)
        return pltpu.make_async_remote_copy(
            src_ref=res_sib.at[span],
            dst_ref=out_ref.at[span, pl.ds(2 * core, 2)],
            send_sem=ret_send.at[piece],
            recv_sem=ret_recv.at[piece],
            device_id={"comp": sib},
            device_id_type=MESH,
        )

    def take_back(piece):
        span = pl.ds(piece * PART, PART)
        return pltpu.make_async_remote_copy(
            src_ref=res_sib.at[span],
            dst_ref=out_ref.at[span, pl.ds(2 * (1 - core), 2)],
            send_sem=ret_send.at[piece],
            recv_sem=ret_recv.at[piece],
            device_id={"comp": sib},
            device_id_type=MESH,
        )

    fetches = [
        pltpu.make_async_copy(source_ref, target_ref, arg_sem.at[place])
        for place, (source_ref, target_ref) in enumerate(
            (
                (lat_any, lat_ref),
                (lon_any, lon_ref),
                (mask_any, mask_ref),
                (strength_any, strength_ref),
                (shift_any, shift_ref),
            )
        )
    ]

    barrier = pltpu.get_barrier_semaphore()

    def greet(**where):
        pl.semaphore_signal(barrier, inc=1, device_id=where, device_id_type=MESH)

    greet(comp=sib)

    @pl.when(has_south)
    def _():
        greet(lat=lat - 1)

    @pl.when(has_north)
    def _():
        greet(lat=lat + 1)

    for far in FAR:

        @pl.when(jnp.logical_and(lat % ROW == 0, lat >= far))
        def _():
            greet(lat=lat - far)

    @pl.when(has_below)
    def _():
        greet(comp=2 * z - 2)
        greet(comp=2 * z - 1)

    @pl.when(has_above)
    def _():
        greet(comp=2 * z + 2)
        greet(comp=2 * z + 3)

    for fetch in fetches:
        fetch.start()
    for ch in range(CHUNKS):
        load(ch).start()

    @pl.when(jnp.logical_not(has_south))
    def _():
        south[...] = jnp.zeros_like(south)
        mask_south[...] = jnp.zeros_like(mask_south)

    @pl.when(jnp.logical_not(has_north))
    def _():
        north[...] = jnp.zeros_like(north)
        mask_north[...] = jnp.zeros_like(mask_north)

    @pl.when(jnp.logical_not(has_below))
    def _():
        g[pl.ds(0, CHIP)] = jnp.zeros((CHIP, 2, 8, 128), jnp.float32)

    @pl.when(jnp.logical_not(has_above))
    def _():
        g[pl.ds(2 * CHIP, CHIP)] = jnp.zeros((CHIP, 2, 8, 128), jnp.float32)

    def one(flag):
        return flag.astype(jnp.int32)

    ahead = sum(one(lat + far < n_lat) for far in FAR) * one(lat % ROW == ROW - 1)
    pl.semaphore_wait(barrier, ahead + 1 + one(has_south) + one(has_north) + 2 * (one(has_below) + one(has_above)))

    @pl.when(has_north)
    def _():
        mask_to_north().start()

    @pl.when(has_south)
    def _():
        mask_to_south().start()

    for ch in range(CHUNKS):

        @pl.when(has_north)
        def _():
            to_north(ch).start()

        @pl.when(has_south)
        def _():
            to_south(ch).start()

    @pl.when(has_south)
    def _():
        mask_to_north().wait_recv()

    @pl.when(has_north)
    def _():
        mask_to_south().wait_recv()

    shape = (4, 8, 128)
    lane = lax.broadcasted_iota(jnp.int32, shape, 2)
    sub = lax.broadcasted_iota(jnp.int32, shape, 1)
    edge_west = lane == 127
    edge_east = lane == 0
    low_sub = sub < 2
    high_sub = sub >= 6
    odd = (sub & 1) == 1

    def other_row(e):
        return jnp.where(odd, pltpu.roll(e, 1, axis=1), pltpu.roll(e, 7, axis=1))

    for fetch in fetches:
        fetch.wait()
    mask = mask_ref[...].astype(jnp.float32)
    base = z * CHIP

    def places(i, carry):
        d = (base + i) & (ND - 1)
        for q in range(NQ):
            place_ref[q, i] = CHIP + i - d + ND * shift_ref[0, q] + ((d + shift_ref[1, q]) & (ND - 1))
        return carry

    lax.fori_loop(0, CHIP, places, 0, unroll=2)

    def advance(ch, carry):
        load(ch).wait()

        @pl.when(has_south)
        def _():
            to_north(ch).wait_recv()

        @pl.when(has_north)
        def _():
            to_south(ch).wait_recv()

        def propagate(j, carry):
            i = ch * STEP + j
            a = lat_ref[i]
            b = lon_ref[i]
            up = a > 0.0
            west_in = b > 0.0
            a = jnp.abs(a)
            b = jnp.abs(b)
            from_halo = odd == up

            def substep(e, upstream, m):
                west, east = roll_lon(e, edge_west, edge_east, low_sub, high_sub)
                side = jnp.where(west_in, west, east)
                moved = e - a * (e - upstream)
                moved = moved - b * (e - side)
                return moved * m

            e = xv[i]
            halo = jnp.where(up, south[i], north[i])
            halo_mask = jnp.where(up, mask_south[...], mask_north[...]).astype(jnp.float32)
            first = substep(e, other_row(jnp.where(from_halo, halo, e)), mask)
            halo = substep(halo, other_row(halo), halo_mask)
            second = substep(first, other_row(jnp.where(from_halo, halo, first)), mask)
            mine = core == 0
            g[CHIP + core * COMP + i] = jnp.where(mine, second[:2], second[2:])
            other[i] = jnp.where(mine, second[2:], second[:2])
            return carry

        lax.fori_loop(0, STEP, propagate, 0, unroll=4)

        for h in range(2):

            @pl.when(has_above)
            def _():
                to_z(0, h, ch).start()

            @pl.when(has_below)
            def _():
                to_z(1, h, ch).start()

        swap(ch).start()
        return carry

    lax.fori_loop(0, CHUNKS, advance, 0)

    for ch in range(CHUNKS):
        swap_in(ch).wait_recv()
        for source_core in range(2):

            @pl.when(has_below)
            def _():
                from_z(0, source_core, ch).wait_recv()

            @pl.when(has_above)
            def _():
                from_z(1, source_core, ch).wait_recv()

    def source(i):
        e = g[CHIP + i]
        total = jnp.zeros_like(e)
        for q in range(NQ):
            partner = g[place_ref[q, i]]
            total = total + partner * (partner - e)
        return e + (strength_ref[base + i] * e) * total

    for piece in range(PIECES):

        def for_sibling(i, carry):
            res_sib[i] = source((1 - core) * COMP + i)
            return carry

        lax.fori_loop(piece * PART, (piece + 1) * PART, for_sibling, 0, unroll=4)
        give_back(piece).start()

    def for_me(i, carry):
        out_ref[i, pl.ds(2 * core, 2)] = source(core * COMP + i)
        return carry

    lax.fori_loop(0, COMP, for_me, 0, unroll=4)

    for ch in range(CHUNKS):

        @pl.when(has_north)
        def _():
            to_north(ch).wait_send()

        @pl.when(has_south)
        def _():
            to_south(ch).wait_send()

        for h in range(2):

            @pl.when(has_above)
            def _():
                to_z(0, h, ch).wait_send()

            @pl.when(has_below)
            def _():
                to_z(1, h, ch).wait_send()

        swap(ch).wait_send()

    @pl.when(has_north)
    def _():
        mask_to_north().wait_send()

    @pl.when(has_south)
    def _():
        mask_to_south().wait_send()

    for piece in range(PIECES):
        give_back(piece).wait_send()
        take_back(piece).wait_recv()


def solution(mesh):
    n_comp, n_lat = mesh.shape["comp"], mesh.shape["lat"]
    block = pltpu.VMEM((COMP, 4, 8, 128), jnp.float32)
    half = pltpu.VMEM((COMP, 2, 8, 128), jnp.float32)
    small = pltpu.VMEM((4, 8, 128), jnp.int32)
    dma = pltpu.SemaphoreType.DMA

    def per_device(spectrum, courant_lat, courant_lon, sea_mask, strength, quad_shift):
        x = spectrum.reshape(COMP, 2, 16, 128).transpose(0, 2, 1, 3).reshape(COMP, 4, 8, 128)
        mask = sea_mask.reshape(2, 16, 128).transpose(1, 0, 2).reshape(4, 8, 128)
        out = pl.pallas_call(
            functools.partial(kernel, n_comp, n_lat),
            out_shape=pltpu.VMEM((COMP, 4, 8, 128), jnp.float32),
            in_specs=[pl.BlockSpec(memory_space=pltpu.HBM)] * 6,
            out_specs=pl.BlockSpec(memory_space=pltpu.VMEM),
            scratch_shapes=[
                pltpu.SMEM((COMP,), jnp.float32),
                pltpu.SMEM((COMP,), jnp.float32),
                pltpu.SMEM((NF * ND,), jnp.float32),
                pltpu.SMEM((2, NQ), jnp.int32),
                pltpu.SMEM((NQ, CHIP), jnp.int32),
                small,
                block,
                block,
                block,
                small,
                small,
                pltpu.VMEM((3 * CHIP, 2, 8, 128), jnp.float32),
                half,
                half,
                dma((5,)),
                dma((CHUNKS,)),
                dma((2, CHUNKS)),
                dma((2, CHUNKS)),
                dma((2,)),
                dma((2,)),
                dma((2, 2, CHUNKS)),
                dma((2, 2, CHUNKS)),
                dma((CHUNKS,)),
                dma((CHUNKS,)),
                dma((PIECES,)),
                dma((PIECES,)),
            ],
            compiler_params=pltpu.CompilerParams(
                collective_id=0, has_side_effects=True, vmem_limit_bytes=VMEM_BYTES
            ),
        )(x, courant_lat, courant_lon, mask, strength, quad_shift.T)
        return out.reshape(COMP, 16, 2, 128).transpose(0, 2, 1, 3).reshape(COMP, 2, 2048)

    return jax.shard_map(
        per_device,
        mesh=mesh,
        in_specs=(P("comp", "lat", None), P("comp"), P("comp"), P("lat", None), P(), P()),
        out_specs=P("comp", "lat", None),
        check_vma=False,
    )
```

```python
import functools

import jax
import jax.numpy as jnp
from jax import lax
from jax.experimental import pallas as pl
from jax.experimental.pallas import tpu as pltpu
from jax.sharding import PartitionSpec as P

NF = 36
ND = 32
NQ = 4
COMP = 72
CHIP = 2 * COMP
CHUNKS = 9
STEP = COMP // CHUNKS
PIECES = 3
PART = COMP // PIECES
VMEM_BYTES = 627 * 1024 * 1024 // 10
ROW = 8
HALF_WAY = 4 * ROW
FAR = (ROW + 1, 2 * ROW + 1, 3 * ROW + 1)

MESH = pl.DeviceIdType.MESH


def roll_lon(e, edge_west, edge_east, low_sub, high_sub):
    down = pltpu.roll(e, 2, axis=1)
    down = jnp.where(low_sub, jnp.concatenate([down[3:], down[:3]], axis=0), down)
    west = pltpu.roll(jnp.where(edge_west, down, e), 1, axis=2)
    up = pltpu.roll(e, 6, axis=1)
    up = jnp.where(high_sub, jnp.concatenate([up[1:], up[:1]], axis=0), up)
    east = pltpu.roll(jnp.where(edge_east, up, e), 127, axis=2)
    return west, east


def kernel(
    n_comp,
    n_lat,
    x_ref,
    lat_any,
    lon_any,
    mask_any,
    strength_any,
    shift_any,
    out_ref,
    lat_ref,
    lon_ref,
    strength_ref,
    shift_ref,
    place_ref,
    mask_ref,
    xv,
    south,
    north,
    mask_south,
    mask_north,
    g,
    other,
    res_sib,
    arg_sem,
    load_sem,
    x_send,
    x_recv,
    m_send,
    m_recv,
    z_send,
    z_recv,
    swap_send,
    swap_recv,
    ret_send,
    ret_recv,
    relay,
):
    comp = lax.axis_index("comp")
    lat = lax.axis_index("lat")
    z = comp // 2
    core = comp % 2
    n_z = n_comp // 2
    has_south = lat > 0
    has_north = lat < n_lat - 1
    has_below = z > 0
    has_above = z < n_z - 1
    sib = z * 2 + 1 - core

    def rows(ch):
        return pl.ds(ch * STEP, STEP)

    def load(ch):
        return pltpu.make_async_copy(x_ref.at[rows(ch)], xv.at[rows(ch)], load_sem.at[ch])

    def to_north(ch):
        return pltpu.make_async_remote_copy(
            src_ref=x_ref.at[rows(ch)],
            dst_ref=south.at[rows(ch)],
            send_sem=x_send.at[0, ch],
            recv_sem=x_recv.at[0, ch],
            device_id={"lat": lat + 1},
            device_id_type=MESH,
        )

    def to_south(ch):
        return pltpu.make_async_remote_copy(
            src_ref=x_ref.at[rows(ch)],
            dst_ref=north.at[rows(ch)],
            send_sem=x_send.at[1, ch],
            recv_sem=x_recv.at[1, ch],
            device_id={"lat": lat - 1},
            device_id_type=MESH,
        )

    def mask_to_north():
        return pltpu.make_async_remote_copy(
            src_ref=mask_any,
            dst_ref=mask_south,
            send_sem=m_send.at[0],
            recv_sem=m_recv.at[0],
            device_id={"lat": lat + 1},
            device_id_type=MESH,
        )

    def mask_to_south():
        return pltpu.make_async_remote_copy(
            src_ref=mask_any,
            dst_ref=mask_north,
            send_sem=m_send.at[1],
            recv_sem=m_recv.at[1],
            device_id={"lat": lat - 1},
            device_id_type=MESH,
        )

    def half_src(h, ch):
        if h == 0:
            return g.at[pl.ds(CHIP + core * COMP + ch * STEP, STEP)]
        return other.at[rows(ch)]

    def to_z(direction, h, ch):
        third = 0 if direction == 0 else 2
        target = (z + 1 if direction == 0 else z - 1) * 2 + (core if h == 0 else 1 - core)
        return pltpu.make_async_remote_copy(
            src_ref=half_src(h, ch),
            dst_ref=g.at[pl.ds(third * CHIP + core * COMP + ch * STEP, STEP)],
            send_sem=z_send.at[direction, h, ch],
            recv_sem=z_recv.at[direction, core, ch],
            device_id={"comp": target},
            device_id_type=MESH,
        )

    def from_z(direction, source_core, ch):
        third = 0 if direction == 0 else 2
        here = g.at[pl.ds(third * CHIP + source_core * COMP + ch * STEP, STEP)]
        return pltpu.make_async_remote_copy(
            src_ref=here,
            dst_ref=here,
            send_sem=z_send.at[direction, 0, ch],
            recv_sem=z_recv.at[direction, source_core, ch],
            device_id={"comp": sib},
            device_id_type=MESH,
        )

    def swap(ch):
        return pltpu.make_async_remote_copy(
            src_ref=other.at[rows(ch)],
            dst_ref=g.at[pl.ds(CHIP + core * COMP + ch * STEP, STEP)],
            send_sem=swap_send.at[ch],
            recv_sem=swap_recv.at[ch],
            device_id={"comp": sib},
            device_id_type=MESH,
        )

    def swap_in(ch):
        here = g.at[pl.ds(CHIP + (1 - core) * COMP + ch * STEP, STEP)]
        return pltpu.make_async_remote_copy(
            src_ref=here,
            dst_ref=here,
            send_sem=swap_send.at[ch],
            recv_sem=swap_recv.at[ch],
            device_id={"comp": sib},
            device_id_type=MESH,
        )

    def give_back(piece):
        span = pl.ds(piece * PART, PART)
        return pltpu.make_async_remote_copy(
            src_ref=res_sib.at[span],
            dst_ref=out_ref.at[span, pl.ds(2 * core, 2)],
            send_sem=ret_send.at[piece],
            recv_sem=ret_recv.at[piece],
            device_id={"comp": sib},
            device_id_type=MESH,
        )

    def take_back(piece):
        span = pl.ds(piece * PART, PART)
        return pltpu.make_async_remote_copy(
            src_ref=res_sib.at[span],
            dst_ref=out_ref.at[span, pl.ds(2 * (1 - core), 2)],
            send_sem=ret_send.at[piece],
            recv_sem=ret_recv.at[piece],
            device_id={"comp": sib},
            device_id_type=MESH,
        )

    fetches = [
        pltpu.make_async_copy(source_ref, target_ref, arg_sem.at[place])
        for place, (source_ref, target_ref) in enumerate(
            (
                (lat_any, lat_ref),
                (lon_any, lon_ref),
                (mask_any, mask_ref),
                (strength_any, strength_ref),
                (shift_any, shift_ref),
            )
        )
    ]

    barrier = pltpu.get_barrier_semaphore()

    def greet(**where):
        pl.semaphore_signal(barrier, inc=1, device_id=where, device_id_type=MESH)

    @pl.when(has_south)
    def _():
        greet(lat=lat - 1)

    @pl.when(has_north)
    def _():
        greet(lat=lat + 1)

    for far in FAR:

        @pl.when(jnp.logical_and(lat % ROW == 0, jnp.logical_and(lat >= far, lat <= HALF_WAY)))
        def _():
            greet(lat=lat - far)

    for fetch in fetches:
        fetch.start()
    for ch in range(CHUNKS):
        load(ch).start()

    @pl.when(jnp.logical_not(has_south))
    def _():
        south[...] = jnp.zeros_like(south)
        mask_south[...] = jnp.zeros_like(mask_south)

    @pl.when(jnp.logical_not(has_north))
    def _():
        north[...] = jnp.zeros_like(north)
        mask_north[...] = jnp.zeros_like(mask_north)

    @pl.when(jnp.logical_not(has_below))
    def _():
        g[pl.ds(0, CHIP)] = jnp.zeros((CHIP, 2, 8, 128), jnp.float32)

    @pl.when(jnp.logical_not(has_above))
    def _():
        g[pl.ds(2 * CHIP, CHIP)] = jnp.zeros((CHIP, 2, 8, 128), jnp.float32)

    def one(flag):
        return flag.astype(jnp.int32)

    near_z = 1 + one(has_below) + one(has_above)
    ahead = sum(one(lat + far <= HALF_WAY) for far in FAR) * one(lat % ROW == ROW - 1)
    odd_core = core == 1
    pl.semaphore_wait(barrier, ahead + one(has_south) + one(has_north) + (1 - core) * near_z)

    @pl.when(odd_core)
    def _():
        greet(comp=2 * z)

        @pl.when(has_below)
        def _():
            greet(comp=2 * z - 2)

        @pl.when(has_above)
        def _():
            greet(comp=2 * z + 2)

    @pl.when(has_north)
    def _():
        mask_to_north().start()

    @pl.when(has_south)
    def _():
        mask_to_south().start()

    for ch in range(CHUNKS):

        @pl.when(has_north)
        def _():
            to_north(ch).start()

        @pl.when(has_south)
        def _():
            to_south(ch).start()

    def tell(target):
        pl.semaphore_signal(relay, inc=1, device_id={"comp": target}, device_id_type=MESH)

    @pl.when(core == 0)
    def _():
        tell(2 * z + 1)

        @pl.when(has_below)
        def _():
            tell(2 * z - 1)

        @pl.when(has_above)
        def _():
            tell(2 * z + 3)

    @pl.when(has_south)
    def _():
        mask_to_north().wait_recv()

    @pl.when(has_north)
    def _():
        mask_to_south().wait_recv()

    shape = (4, 8, 128)
    lane = lax.broadcasted_iota(jnp.int32, shape, 2)
    sub = lax.broadcasted_iota(jnp.int32, shape, 1)
    edge_west = lane == 127
    edge_east = lane == 0
    low_sub = sub < 2
    high_sub = sub >= 6
    odd = (sub & 1) == 1

    def other_row(e):
        return jnp.where(odd, pltpu.roll(e, 1, axis=1), pltpu.roll(e, 7, axis=1))

    for fetch in fetches:
        fetch.wait()
    mask = mask_ref[...].astype(jnp.float32)
    base = z * CHIP

    def places(i, carry):
        d = (base + i) & (ND - 1)
        for q in range(NQ):
            place_ref[q, i] = CHIP + i - d + ND * shift_ref[0, q] + ((d + shift_ref[1, q]) & (ND - 1))
        return carry

    lax.fori_loop(0, CHIP, places, 0, unroll=2)

    pl.semaphore_wait(relay, jnp.where(odd_core, near_z, 1))

    @pl.when(odd_core)
    def _():
        tell(2 * z)

    def advance(ch, carry):
        load(ch).wait()

        @pl.when(has_south)
        def _():
            to_north(ch).wait_recv()

        @pl.when(has_north)
        def _():
            to_south(ch).wait_recv()

        def propagate(j, carry):
            i = ch * STEP + j
            a = lat_ref[i]
            b = lon_ref[i]
            up = a > 0.0
            west_in = b > 0.0
            a = jnp.abs(a)
            b = jnp.abs(b)
            from_halo = odd == up

            def substep(e, upstream, m):
                west, east = roll_lon(e, edge_west, edge_east, low_sub, high_sub)
                side = jnp.where(west_in, west, east)
                moved = e - a * (e - upstream)
                moved = moved - b * (e - side)
                return moved * m

            e = xv[i]
            halo = jnp.where(up, south[i], north[i])
            halo_mask = jnp.where(up, mask_south[...], mask_north[...]).astype(jnp.float32)
            first = substep(e, other_row(jnp.where(from_halo, halo, e)), mask)
            halo = substep(halo, other_row(halo), halo_mask)
            second = substep(first, other_row(jnp.where(from_halo, halo, first)), mask)
            mine = core == 0
            g[CHIP + core * COMP + i] = jnp.where(mine, second[:2], second[2:])
            other[i] = jnp.where(mine, second[2:], second[:2])
            return carry

        lax.fori_loop(0, STEP, propagate, 0, unroll=4)

        for h in range(2):

            @pl.when(has_above)
            def _():
                to_z(0, h, ch).start()

            @pl.when(has_below)
            def _():
                to_z(1, h, ch).start()

        swap(ch).start()
        return carry

    lax.fori_loop(0, CHUNKS, advance, 0)

    for ch in range(CHUNKS):
        swap_in(ch).wait_recv()
        for source_core in range(2):

            @pl.when(has_below)
            def _():
                from_z(0, source_core, ch).wait_recv()

            @pl.when(has_above)
            def _():
                from_z(1, source_core, ch).wait_recv()

    def source(i):
        e = g[CHIP + i]
        total = jnp.zeros_like(e)
        for q in range(NQ):
            partner = g[place_ref[q, i]]
            total = total + partner * (partner - e)
        return e + (strength_ref[base + i] * e) * total

    for piece in range(PIECES):

        def for_sibling(i, carry):
            res_sib[i] = source((1 - core) * COMP + i)
            return carry

        lax.fori_loop(piece * PART, (piece + 1) * PART, for_sibling, 0, unroll=4)
        give_back(piece).start()

    def for_me(i, carry):
        out_ref[i, pl.ds(2 * core, 2)] = source(core * COMP + i)
        return carry

    lax.fori_loop(0, COMP, for_me, 0, unroll=4)

    for ch in range(CHUNKS):

        @pl.when(has_north)
        def _():
            to_north(ch).wait_send()

        @pl.when(has_south)
        def _():
            to_south(ch).wait_send()

        for h in range(2):

            @pl.when(has_above)
            def _():
                to_z(0, h, ch).wait_send()

            @pl.when(has_below)
            def _():
                to_z(1, h, ch).wait_send()

        swap(ch).wait_send()

    @pl.when(has_north)
    def _():
        mask_to_north().wait_send()

    @pl.when(has_south)
    def _():
        mask_to_south().wait_send()

    for piece in range(PIECES):
        give_back(piece).wait_send()
        take_back(piece).wait_recv()


def solution(mesh):
    n_comp, n_lat = mesh.shape["comp"], mesh.shape["lat"]
    block = pltpu.VMEM((COMP, 4, 8, 128), jnp.float32)
    half = pltpu.VMEM((COMP, 2, 8, 128), jnp.float32)
    small = pltpu.VMEM((4, 8, 128), jnp.int32)
    dma = pltpu.SemaphoreType.DMA

    def per_device(spectrum, courant_lat, courant_lon, sea_mask, strength, quad_shift):
        x = spectrum.reshape(COMP, 2, 16, 128).transpose(0, 2, 1, 3).reshape(COMP, 4, 8, 128)
        mask = sea_mask.reshape(2, 16, 128).transpose(1, 0, 2).reshape(4, 8, 128)
        out = pl.pallas_call(
            functools.partial(kernel, n_comp, n_lat),
            out_shape=pltpu.VMEM((COMP, 4, 8, 128), jnp.float32),
            in_specs=[pl.BlockSpec(memory_space=pltpu.HBM)] * 6,
            out_specs=pl.BlockSpec(memory_space=pltpu.VMEM),
            scratch_shapes=[
                pltpu.SMEM((COMP,), jnp.float32),
                pltpu.SMEM((COMP,), jnp.float32),
                pltpu.SMEM((NF * ND,), jnp.float32),
                pltpu.SMEM((2, NQ), jnp.int32),
                pltpu.SMEM((NQ, CHIP), jnp.int32),
                small,
                block,
                block,
                block,
                small,
                small,
                pltpu.VMEM((3 * CHIP, 2, 8, 128), jnp.float32),
                half,
                half,
                dma((5,)),
                dma((CHUNKS,)),
                dma((2, CHUNKS)),
                dma((2, CHUNKS)),
                dma((2,)),
                dma((2,)),
                dma((2, 2, CHUNKS)),
                dma((2, 2, CHUNKS)),
                dma((CHUNKS,)),
                dma((CHUNKS,)),
                dma((PIECES,)),
                dma((PIECES,)),
                pltpu.SemaphoreType.REGULAR,
            ],
            compiler_params=pltpu.CompilerParams(
                collective_id=0, has_side_effects=True, vmem_limit_bytes=VMEM_BYTES
            ),
        )(x, courant_lat, courant_lon, mask, strength, quad_shift.T)
        return out.reshape(COMP, 16, 2, 128).transpose(0, 2, 1, 3).reshape(COMP, 2, 2048)

    return jax.shard_map(
        per_device,
        mesh=mesh,
        in_specs=(P("comp", "lat", None), P("comp"), P("comp"), P("lat", None), P(), P()),
        out_specs=P("comp", "lat", None),
        check_vma=False,
    )
```

```python
import functools

import jax
import jax.numpy as jnp
from jax import lax
from jax.experimental import pallas as pl
from jax.experimental.pallas import tpu as pltpu
from jax.sharding import PartitionSpec as P

NF = 36
ND = 32
NQ = 4
COMP = 72
CHIP = 2 * COMP
EDGE = 4
STEP = 8
MIDDLE = (COMP - 2 * EDGE) // STEP
EARLY = 2
CHUNKS = MIDDLE + 2
PIECES = 3
PART = COMP // PIECES
VMEM_BYTES = 627 * 1024 * 1024 // 10
ROW = 8
HALF_WAY = 4 * ROW
FAR = (ROW + 1, 2 * ROW + 1, 3 * ROW + 1)

MESH = pl.DeviceIdType.MESH


def roll_lon(e, edge_west, edge_east, low_sub, high_sub):
    down = pltpu.roll(e, 2, axis=1)
    down = jnp.where(low_sub, jnp.concatenate([down[3:], down[:3]], axis=0), down)
    west = pltpu.roll(jnp.where(edge_west, down, e), 1, axis=2)
    up = pltpu.roll(e, 6, axis=1)
    up = jnp.where(high_sub, jnp.concatenate([up[1:], up[:1]], axis=0), up)
    east = pltpu.roll(jnp.where(edge_east, up, e), 127, axis=2)
    return west, east


def kernel(
    n_comp,
    n_lat,
    x_ref,
    lat_any,
    lon_any,
    mask_any,
    strength_any,
    shift_any,
    out_ref,
    lat_ref,
    lon_ref,
    strength_ref,
    shift_ref,
    place_ref,
    mask_ref,
    xv,
    south,
    north,
    mask_south,
    mask_north,
    g,
    other,
    res_sib,
    arg_sem,
    load_sem,
    x_send,
    x_recv,
    m_send,
    m_recv,
    z_send,
    z_recv,
    swap_send,
    swap_recv,
    ret_send,
    ret_recv,
    relay,
):
    comp = lax.axis_index("comp")
    lat = lax.axis_index("lat")
    z = comp // 2
    core = comp % 2
    n_z = n_comp // 2
    has_south = lat > 0
    has_north = lat < n_lat - 1
    has_below = z > 0
    has_above = z < n_z - 1
    sib = z * 2 + 1 - core
    odd_core = core == 1

    first_chunk = (0, 0, EDGE)
    last_chunk = (CHUNKS - 1, COMP - EDGE, EDGE)

    def middle_chunk(k):
        return (k + 1, EDGE + STEP * k, STEP)

    def each_chunk(act):
        act(first_chunk)

        def step(k, carry):
            act(middle_chunk(k))
            return carry

        lax.fori_loop(0, MIDDLE, step, 0)
        act(last_chunk)

    def span_at(offset, ch):
        return pl.ds(offset + ch[1], ch[2])

    def rows(ch):
        return span_at(0, ch)

    load = pltpu.make_async_copy(x_ref, xv, load_sem)

    def to_north(ch):
        return pltpu.make_async_remote_copy(
            src_ref=x_ref.at[rows(ch)],
            dst_ref=south.at[rows(ch)],
            send_sem=x_send.at[0, ch[0]],
            recv_sem=x_recv.at[0, ch[0]],
            device_id={"lat": lat + 1},
            device_id_type=MESH,
        )

    def to_south(ch):
        return pltpu.make_async_remote_copy(
            src_ref=x_ref.at[rows(ch)],
            dst_ref=north.at[rows(ch)],
            send_sem=x_send.at[1, ch[0]],
            recv_sem=x_recv.at[1, ch[0]],
            device_id={"lat": lat - 1},
            device_id_type=MESH,
        )

    def mask_to_north():
        return pltpu.make_async_remote_copy(
            src_ref=mask_any,
            dst_ref=mask_south,
            send_sem=m_send.at[0],
            recv_sem=m_recv.at[0],
            device_id={"lat": lat + 1},
            device_id_type=MESH,
        )

    def mask_to_south():
        return pltpu.make_async_remote_copy(
            src_ref=mask_any,
            dst_ref=mask_north,
            send_sem=m_send.at[1],
            recv_sem=m_recv.at[1],
            device_id={"lat": lat - 1},
            device_id_type=MESH,
        )

    def half_src(h, ch):
        if h == 0:
            return g.at[span_at(CHIP + core * COMP, ch)]
        return other.at[rows(ch)]

    def to_z(direction, h, ch):
        third = 0 if direction == 0 else 2
        target = (z + 1 if direction == 0 else z - 1) * 2 + (core if h == 0 else 1 - core)
        return pltpu.make_async_remote_copy(
            src_ref=half_src(h, ch),
            dst_ref=g.at[span_at(third * CHIP + core * COMP, ch)],
            send_sem=z_send.at[direction, h, ch[0]],
            recv_sem=z_recv.at[direction, core, ch[0]],
            device_id={"comp": target},
            device_id_type=MESH,
        )

    def skipped(direction, parity, source_core, ch):
        if direction == 0:
            first = jnp.where(parity == 0, 4, 0)
            last = 12
            owner = 0
        else:
            first = 60
            last = jnp.where(parity == 0, 72, 68)
            owner = 1
        start = ch[1]
        return jnp.logical_and(source_core == owner, jnp.logical_and(start >= first, start < last))

    def sends_up(ch):
        return jnp.logical_and(has_above, jnp.logical_not(skipped(0, z % 2, core, ch)))

    def sends_down(ch):
        return jnp.logical_and(has_below, jnp.logical_not(skipped(1, z % 2, core, ch)))

    def comes_up(source_core, ch):
        return jnp.logical_and(has_below, jnp.logical_not(skipped(0, (z + 1) % 2, source_core, ch)))

    def comes_down(source_core, ch):
        return jnp.logical_and(has_above, jnp.logical_not(skipped(1, (z + 1) % 2, source_core, ch)))

    def from_z(direction, source_core, ch):
        third = 0 if direction == 0 else 2
        here = g.at[span_at(third * CHIP + source_core * COMP, ch)]
        return pltpu.make_async_remote_copy(
            src_ref=here,
            dst_ref=here,
            send_sem=z_send.at[direction, 0, ch[0]],
            recv_sem=z_recv.at[direction, source_core, ch[0]],
            device_id={"comp": sib},
            device_id_type=MESH,
        )

    def swap(ch):
        return pltpu.make_async_remote_copy(
            src_ref=other.at[rows(ch)],
            dst_ref=g.at[span_at(CHIP + core * COMP, ch)],
            send_sem=swap_send.at[ch[0]],
            recv_sem=swap_recv.at[ch[0]],
            device_id={"comp": sib},
            device_id_type=MESH,
        )

    def swap_in(ch):
        here = g.at[span_at(CHIP + (1 - core) * COMP, ch)]
        return pltpu.make_async_remote_copy(
            src_ref=here,
            dst_ref=here,
            send_sem=swap_send.at[ch[0]],
            recv_sem=swap_recv.at[ch[0]],
            device_id={"comp": sib},
            device_id_type=MESH,
        )

    def give_back(piece):
        span = pl.ds(piece * PART, PART)
        return pltpu.make_async_remote_copy(
            src_ref=res_sib.at[span],
            dst_ref=out_ref.at[span, pl.ds(2 * core, 2)],
            send_sem=ret_send.at[piece],
            recv_sem=ret_recv.at[piece],
            device_id={"comp": sib},
            device_id_type=MESH,
        )

    def take_back(piece):
        span = pl.ds(piece * PART, PART)
        return pltpu.make_async_remote_copy(
            src_ref=res_sib.at[span],
            dst_ref=out_ref.at[span, pl.ds(2 * (1 - core), 2)],
            send_sem=ret_send.at[piece],
            recv_sem=ret_recv.at[piece],
            device_id={"comp": sib},
            device_id_type=MESH,
        )

    fetches = [
        pltpu.make_async_copy(source_ref, target_ref, arg_sem.at[place])
        for place, (source_ref, target_ref) in enumerate(
            (
                (lat_any, lat_ref),
                (lon_any, lon_ref),
                (mask_any, mask_ref),
                (strength_any, strength_ref),
                (shift_any, shift_ref),
            )
        )
    ]

    barrier = pltpu.get_barrier_semaphore()

    def greet(**where):
        pl.semaphore_signal(barrier, inc=1, device_id=where, device_id_type=MESH)

    @pl.when(odd_core)
    def _():
        greet(comp=sib)

    @pl.when(has_below)
    def _():
        greet(comp=2 * z - 2)

    @pl.when(has_south)
    def _():
        greet(lat=lat - 1)

    @pl.when(has_north)
    def _():
        greet(lat=lat + 1)

    for far in FAR:

        @pl.when(jnp.logical_and(jnp.logical_and(core == 0, lat % ROW == 0), jnp.logical_and(lat >= far, lat <= HALF_WAY)))
        def _():
            greet(lat=lat - far)

    for fetch in fetches:
        fetch.start()
    load.start()

    @pl.when(jnp.logical_not(has_south))
    def _():
        south[...] = jnp.zeros_like(south)
        mask_south[...] = jnp.zeros_like(mask_south)

    @pl.when(jnp.logical_not(has_north))
    def _():
        north[...] = jnp.zeros_like(north)
        mask_north[...] = jnp.zeros_like(mask_north)

    @pl.when(jnp.logical_not(has_below))
    def _():
        g[pl.ds(0, CHIP)] = jnp.zeros((CHIP, 2, 8, 128), jnp.float32)

    @pl.when(jnp.logical_not(has_above))
    def _():
        g[pl.ds(2 * CHIP, CHIP)] = jnp.zeros((CHIP, 2, 8, 128), jnp.float32)

    def one(flag):
        return flag.astype(jnp.int32)

    ahead = sum(one(lat + far <= HALF_WAY) for far in FAR) * one(lat % ROW == ROW - 1)
    held_back = jnp.logical_and(odd_core, ahead > 0)
    line = one(has_south) + one(has_north)
    pl.semaphore_wait(barrier, line + (1 - core) * (ahead + 1 + 2 * one(has_above)))

    def tell(target):
        pl.semaphore_signal(relay, inc=1, device_id={"comp": target}, device_id_type=MESH)

    @pl.when(core == 0)
    def _():
        tell(2 * z + 1)

        @pl.when(has_above)
        def _():
            tell(2 * z + 2)
            tell(2 * z + 3)

    @pl.when(has_north)
    def _():
        mask_to_north().start()

    @pl.when(has_south)
    def _():
        mask_to_south().start()

    def send_rows(ch):
        @pl.when(jnp.logical_and(has_north, jnp.logical_or(jnp.logical_not(held_back), ch[0] <= EARLY)))
        def _():
            to_north(ch).start()

        @pl.when(has_south)
        def _():
            to_south(ch).start()

    def send_rest(ch):
        @pl.when(jnp.logical_and(held_back, ch[0] > EARLY))
        def _():
            to_north(ch).start()

    each_chunk(send_rows)

    @pl.when(has_south)
    def _():
        mask_to_north().wait_recv()

    @pl.when(has_north)
    def _():
        mask_to_south().wait_recv()

    shape = (4, 8, 128)
    lane = lax.broadcasted_iota(jnp.int32, shape, 2)
    sub = lax.broadcasted_iota(jnp.int32, shape, 1)
    edge_west = lane == 127
    edge_east = lane == 0
    low_sub = sub < 2
    high_sub = sub >= 6
    odd = (sub & 1) == 1

    def other_row(e):
        return jnp.where(odd, pltpu.roll(e, 1, axis=1), pltpu.roll(e, 7, axis=1))

    for fetch in fetches:
        fetch.wait()
    mask = mask_ref[...].astype(jnp.float32)
    base = z * CHIP

    def places(i, carry):
        d = (base + i) & (ND - 1)
        for q in range(NQ):
            place_ref[q, i] = CHIP + i - d + ND * shift_ref[0, q] + ((d + shift_ref[1, q]) & (ND - 1))
        return carry

    lax.fori_loop(0, CHIP, places, 0, unroll=2)

    @pl.when(jnp.logical_or(odd_core, has_below))
    def _():
        pl.semaphore_wait(relay, core + one(has_below))

    each_chunk(send_rest)

    load.wait()

    def advance(ch):
        @pl.when(has_south)
        def _():
            to_north(ch).wait_recv()

        @pl.when(has_north)
        def _():
            to_south(ch).wait_recv()

        def propagate(j, carry):
            i = ch[1] + j
            a = lat_ref[i]
            b = lon_ref[i]
            up = a > 0.0
            west_in = b > 0.0
            a = jnp.abs(a)
            b = jnp.abs(b)
            from_halo = odd == up

            def substep(e, upstream, m):
                west, east = roll_lon(e, edge_west, edge_east, low_sub, high_sub)
                side = jnp.where(west_in, west, east)
                moved = e - a * (e - upstream)
                moved = moved - b * (e - side)
                return moved * m

            e = xv[i]
            halo = jnp.where(up, south[i], north[i])
            halo_mask = jnp.where(up, mask_south[...], mask_north[...]).astype(jnp.float32)
            first = substep(e, other_row(jnp.where(from_halo, halo, e)), mask)
            halo = substep(halo, other_row(halo), halo_mask)
            second = substep(first, other_row(jnp.where(from_halo, halo, first)), mask)
            mine = core == 0
            g[CHIP + core * COMP + i] = jnp.where(mine, second[:2], second[2:])
            other[i] = jnp.where(mine, second[2:], second[:2])
            return carry

        lax.fori_loop(0, ch[2], propagate, 0, unroll=4)

        for h in range(2):

            @pl.when(sends_up(ch))
            def _():
                to_z(0, h, ch).start()

            @pl.when(sends_down(ch))
            def _():
                to_z(1, h, ch).start()

        swap(ch).start()

    each_chunk(advance)

    def arrive(ch):
        swap_in(ch).wait_recv()
        for source_core in range(2):

            @pl.when(comes_up(source_core, ch))
            def _():
                from_z(0, source_core, ch).wait_recv()

            @pl.when(comes_down(source_core, ch))
            def _():
                from_z(1, source_core, ch).wait_recv()

    each_chunk(arrive)

    def source(i):
        e = g[CHIP + i]
        total = jnp.zeros_like(e)
        for q in range(NQ):
            partner = g[place_ref[q, i]]
            total = total + partner * (partner - e)
        return e + (strength_ref[base + i] * e) * total

    for piece in range(PIECES):

        def for_sibling(i, carry):
            res_sib[i] = source((1 - core) * COMP + i)
            return carry

        lax.fori_loop(piece * PART, (piece + 1) * PART, for_sibling, 0, unroll=4)
        give_back(piece).start()

    def for_me(i, carry):
        out_ref[i, pl.ds(2 * core, 2)] = source(core * COMP + i)
        return carry

    lax.fori_loop(0, COMP, for_me, 0, unroll=4)

    def left(ch):
        @pl.when(has_north)
        def _():
            to_north(ch).wait_send()

        @pl.when(has_south)
        def _():
            to_south(ch).wait_send()

        for h in range(2):

            @pl.when(sends_up(ch))
            def _():
                to_z(0, h, ch).wait_send()

            @pl.when(sends_down(ch))
            def _():
                to_z(1, h, ch).wait_send()

        swap(ch).wait_send()

    each_chunk(left)

    @pl.when(has_north)
    def _():
        mask_to_north().wait_send()

    @pl.when(has_south)
    def _():
        mask_to_south().wait_send()

    for piece in range(PIECES):
        give_back(piece).wait_send()
        take_back(piece).wait_recv()


def solution(mesh):
    n_comp, n_lat = mesh.shape["comp"], mesh.shape["lat"]
    block = pltpu.VMEM((COMP, 4, 8, 128), jnp.float32)
    half = pltpu.VMEM((COMP, 2, 8, 128), jnp.float32)
    small = pltpu.VMEM((4, 8, 128), jnp.int32)
    dma = pltpu.SemaphoreType.DMA

    def per_device(spectrum, courant_lat, courant_lon, sea_mask, strength, quad_shift):
        x = spectrum.reshape(COMP, 2, 16, 128).transpose(0, 2, 1, 3).reshape(COMP, 4, 8, 128)
        mask = sea_mask.reshape(2, 16, 128).transpose(1, 0, 2).reshape(4, 8, 128)
        out = pl.pallas_call(
            functools.partial(kernel, n_comp, n_lat),
            out_shape=pltpu.VMEM((COMP, 4, 8, 128), jnp.float32),
            in_specs=[pl.BlockSpec(memory_space=pltpu.HBM)] * 6,
            out_specs=pl.BlockSpec(memory_space=pltpu.VMEM),
            scratch_shapes=[
                pltpu.SMEM((COMP,), jnp.float32),
                pltpu.SMEM((COMP,), jnp.float32),
                pltpu.SMEM((NF * ND,), jnp.float32),
                pltpu.SMEM((2, NQ), jnp.int32),
                pltpu.SMEM((NQ, CHIP), jnp.int32),
                small,
                block,
                block,
                block,
                small,
                small,
                pltpu.VMEM((3 * CHIP, 2, 8, 128), jnp.float32),
                half,
                half,
                dma((5,)),
                dma,
                dma((2, CHUNKS)),
                dma((2, CHUNKS)),
                dma((2,)),
                dma((2,)),
                dma((2, 2, CHUNKS)),
                dma((2, 2, CHUNKS)),
                dma((CHUNKS,)),
                dma((CHUNKS,)),
                dma((PIECES,)),
                dma((PIECES,)),
                pltpu.SemaphoreType.REGULAR,
            ],
            compiler_params=pltpu.CompilerParams(
                collective_id=0, has_side_effects=True, vmem_limit_bytes=VMEM_BYTES
            ),
        )(x, courant_lat, courant_lon, mask, strength, quad_shift.T)
        return out.reshape(COMP, 16, 2, 128).transpose(0, 2, 1, 3).reshape(COMP, 2, 2048)

    return jax.shard_map(
        per_device,
        mesh=mesh,
        in_specs=(P("comp", "lat", None), P("comp"), P("comp"), P("lat", None), P(), P()),
        out_specs=P("comp", "lat", None),
        check_vma=False,
    )
```

```python
import functools

import jax
import jax.numpy as jnp
from jax import lax
from jax.experimental import pallas as pl
from jax.experimental.pallas import tpu as pltpu
from jax.sharding import PartitionSpec as P

NF = 36
ND = 32
NQ = 4
COMP = 72
CHIP = 2 * COMP
EDGE = 4
STEP = 8
MIDDLE = (COMP - 2 * EDGE) // STEP
EARLY = 2
CHUNKS = MIDDLE + 2
PIECES = 3
PART = COMP // PIECES
VMEM_BYTES = 627 * 1024 * 1024 // 10
ROW = 8
HALF_WAY = 4 * ROW
FAR = (ROW + 1, 2 * ROW + 1, 3 * ROW + 1)

MESH = pl.DeviceIdType.MESH


def roll_lon(e, edge_west, edge_east, low_sub, high_sub):
    down = pltpu.roll(e, 2, axis=1)
    down = jnp.where(low_sub, jnp.concatenate([down[3:], down[:3]], axis=0), down)
    west = pltpu.roll(jnp.where(edge_west, down, e), 1, axis=2)
    up = pltpu.roll(e, 6, axis=1)
    up = jnp.where(high_sub, jnp.concatenate([up[1:], up[:1]], axis=0), up)
    east = pltpu.roll(jnp.where(edge_east, up, e), 127, axis=2)
    return west, east


def kernel(
    n_comp,
    n_lat,
    x_ref,
    lat_any,
    lon_any,
    mask_any,
    strength_any,
    shift_any,
    out_ref,
    lat_ref,
    lon_ref,
    strength_ref,
    shift_ref,
    place_ref,
    mask_ref,
    xv,
    south,
    north,
    mask_south,
    mask_north,
    g,
    other,
    res_sib,
    arg_sem,
    load_sem,
    x_send,
    x_recv,
    m_send,
    m_recv,
    z_send,
    z_recv,
    swap_send,
    swap_recv,
    ret_send,
    ret_recv,
    relay,
):
    comp = lax.axis_index("comp")
    lat = lax.axis_index("lat")
    z = comp // 2
    core = comp % 2
    n_z = n_comp // 2
    has_south = lat > 0
    has_north = lat < n_lat - 1
    has_below = z > 0
    has_above = z < n_z - 1
    sib = z * 2 + 1 - core
    odd_core = core == 1

    first_chunk = (0, 0, EDGE)
    last_chunk = (CHUNKS - 1, COMP - EDGE, EDGE)

    def middle_chunk(k):
        return (k + 1, EDGE + STEP * k, STEP)

    def each_chunk(act):
        act(first_chunk)

        def step(k, carry):
            act(middle_chunk(k))
            return carry

        lax.fori_loop(0, MIDDLE, step, 0)
        act(last_chunk)

    def span_at(offset, ch):
        return pl.ds(offset + ch[1], ch[2])

    def rows(ch):
        return span_at(0, ch)

    load = pltpu.make_async_copy(x_ref, xv, load_sem)

    def to_north(ch):
        return pltpu.make_async_remote_copy(
            src_ref=x_ref.at[rows(ch)],
            dst_ref=south.at[rows(ch)],
            send_sem=x_send.at[0, ch[0]],
            recv_sem=x_recv.at[0, ch[0]],
            device_id={"lat": lat + 1},
            device_id_type=MESH,
        )

    def to_south(ch):
        return pltpu.make_async_remote_copy(
            src_ref=x_ref.at[rows(ch)],
            dst_ref=north.at[rows(ch)],
            send_sem=x_send.at[1, ch[0]],
            recv_sem=x_recv.at[1, ch[0]],
            device_id={"lat": lat - 1},
            device_id_type=MESH,
        )

    def mask_to_north():
        return pltpu.make_async_remote_copy(
            src_ref=mask_any,
            dst_ref=mask_south,
            send_sem=m_send.at[0],
            recv_sem=m_recv.at[0],
            device_id={"lat": lat + 1},
            device_id_type=MESH,
        )

    def mask_to_south():
        return pltpu.make_async_remote_copy(
            src_ref=mask_any,
            dst_ref=mask_north,
            send_sem=m_send.at[1],
            recv_sem=m_recv.at[1],
            device_id={"lat": lat - 1},
            device_id_type=MESH,
        )

    def half_src(h, ch):
        if h == 0:
            return g.at[span_at(CHIP + core * COMP, ch)]
        return other.at[rows(ch)]

    def to_z(direction, h, ch):
        third = 0 if direction == 0 else 2
        target = (z + 1 if direction == 0 else z - 1) * 2 + (core if h == 0 else 1 - core)
        return pltpu.make_async_remote_copy(
            src_ref=half_src(h, ch),
            dst_ref=g.at[span_at(third * CHIP + core * COMP, ch)],
            send_sem=z_send.at[direction, h, ch[0]],
            recv_sem=z_recv.at[direction, core, ch[0]],
            device_id={"comp": target},
            device_id_type=MESH,
        )

    def skipped(direction, parity, source_core, ch):
        if direction == 0:
            first = jnp.where(parity == 0, 4, 0)
            last = 12
            owner = 0
        else:
            first = 60
            last = jnp.where(parity == 0, 72, 68)
            owner = 1
        start = ch[1]
        return jnp.logical_and(source_core == owner, jnp.logical_and(start >= first, start < last))

    def sends_up(ch):
        return jnp.logical_and(has_above, jnp.logical_not(skipped(0, z % 2, core, ch)))

    def sends_down(ch):
        return jnp.logical_and(has_below, jnp.logical_not(skipped(1, z % 2, core, ch)))

    def comes_up(source_core, ch):
        return jnp.logical_and(has_below, jnp.logical_not(skipped(0, (z + 1) % 2, source_core, ch)))

    def comes_down(source_core, ch):
        return jnp.logical_and(has_above, jnp.logical_not(skipped(1, (z + 1) % 2, source_core, ch)))

    def from_z(direction, source_core, ch):
        third = 0 if direction == 0 else 2
        here = g.at[span_at(third * CHIP + source_core * COMP, ch)]
        return pltpu.make_async_remote_copy(
            src_ref=here,
            dst_ref=here,
            send_sem=z_send.at[direction, 0, ch[0]],
            recv_sem=z_recv.at[direction, source_core, ch[0]],
            device_id={"comp": sib},
            device_id_type=MESH,
        )

    def swap(ch):
        return pltpu.make_async_remote_copy(
            src_ref=other.at[rows(ch)],
            dst_ref=g.at[span_at(CHIP + core * COMP, ch)],
            send_sem=swap_send.at[ch[0]],
            recv_sem=swap_recv.at[ch[0]],
            device_id={"comp": sib},
            device_id_type=MESH,
        )

    def swap_in(ch):
        here = g.at[span_at(CHIP + (1 - core) * COMP, ch)]
        return pltpu.make_async_remote_copy(
            src_ref=here,
            dst_ref=here,
            send_sem=swap_send.at[ch[0]],
            recv_sem=swap_recv.at[ch[0]],
            device_id={"comp": sib},
            device_id_type=MESH,
        )

    def give_back(piece):
        span = pl.ds(piece * PART, PART)
        return pltpu.make_async_remote_copy(
            src_ref=res_sib.at[span],
            dst_ref=out_ref.at[span, pl.ds(2 * core, 2)],
            send_sem=ret_send.at[piece],
            recv_sem=ret_recv.at[piece],
            device_id={"comp": sib},
            device_id_type=MESH,
        )

    def take_back(piece):
        span = pl.ds(piece * PART, PART)
        return pltpu.make_async_remote_copy(
            src_ref=res_sib.at[span],
            dst_ref=out_ref.at[span, pl.ds(2 * (1 - core), 2)],
            send_sem=ret_send.at[piece],
            recv_sem=ret_recv.at[piece],
            device_id={"comp": sib},
            device_id_type=MESH,
        )

    fetches = [
        pltpu.make_async_copy(source_ref, target_ref, arg_sem.at[place])
        for place, (source_ref, target_ref) in enumerate(
            (
                (lat_any, lat_ref),
                (lon_any, lon_ref),
                (mask_any, mask_ref),
                (strength_any, strength_ref),
                (shift_any, shift_ref),
            )
        )
    ]

    barrier = pltpu.get_barrier_semaphore()

    def greet(**where):
        pl.semaphore_signal(barrier, inc=1, device_id=where, device_id_type=MESH)

    @pl.when(odd_core)
    def _():
        greet(comp=sib)

    @pl.when(has_above)
    def _():
        greet(comp=2 * z + 2)

    @pl.when(has_south)
    def _():
        greet(lat=lat - 1)

    @pl.when(has_north)
    def _():
        greet(lat=lat + 1)

    for far in FAR:

        @pl.when(jnp.logical_and(jnp.logical_and(core == 0, lat % ROW == 0), jnp.logical_and(lat >= far, lat <= HALF_WAY)))
        def _():
            greet(lat=lat - far)

    for fetch in fetches:
        fetch.start()
    load.start()

    @pl.when(jnp.logical_not(has_south))
    def _():
        south[...] = jnp.zeros_like(south)
        mask_south[...] = jnp.zeros_like(mask_south)

    @pl.when(jnp.logical_not(has_north))
    def _():
        north[...] = jnp.zeros_like(north)
        mask_north[...] = jnp.zeros_like(mask_north)

    @pl.when(jnp.logical_not(has_below))
    def _():
        g[pl.ds(0, CHIP)] = jnp.zeros((CHIP, 2, 8, 128), jnp.float32)

    @pl.when(jnp.logical_not(has_above))
    def _():
        g[pl.ds(2 * CHIP, CHIP)] = jnp.zeros((CHIP, 2, 8, 128), jnp.float32)

    def one(flag):
        return flag.astype(jnp.int32)

    ahead = sum(one(lat + far <= HALF_WAY) for far in FAR) * one(lat % ROW == ROW - 1)
    held_back = jnp.logical_and(odd_core, ahead > 0)
    line = one(has_south) + one(has_north)
    pl.semaphore_wait(barrier, line + (1 - core) * (ahead + 1 + 2 * one(has_below)))

    def tell(target):
        pl.semaphore_signal(relay, inc=1, device_id={"comp": target}, device_id_type=MESH)

    @pl.when(core == 0)
    def _():
        tell(2 * z + 1)

        @pl.when(has_below)
        def _():
            tell(2 * z - 2)
            tell(2 * z - 1)

    @pl.when(has_north)
    def _():
        mask_to_north().start()

    @pl.when(has_south)
    def _():
        mask_to_south().start()

    def send_rows(ch):
        @pl.when(jnp.logical_and(has_north, jnp.logical_or(jnp.logical_not(held_back), ch[0] <= EARLY)))
        def _():
            to_north(ch).start()

        @pl.when(has_south)
        def _():
            to_south(ch).start()

    def send_rest(ch):
        @pl.when(jnp.logical_and(held_back, ch[0] > EARLY))
        def _():
            to_north(ch).start()

    each_chunk(send_rows)

    @pl.when(has_south)
    def _():
        mask_to_north().wait_recv()

    @pl.when(has_north)
    def _():
        mask_to_south().wait_recv()

    shape = (4, 8, 128)
    lane = lax.broadcasted_iota(jnp.int32, shape, 2)
    sub = lax.broadcasted_iota(jnp.int32, shape, 1)
    edge_west = lane == 127
    edge_east = lane == 0
    low_sub = sub < 2
    high_sub = sub >= 6
    odd = (sub & 1) == 1

    def other_row(e):
        return jnp.where(odd, pltpu.roll(e, 1, axis=1), pltpu.roll(e, 7, axis=1))

    for fetch in fetches:
        fetch.wait()
    mask = mask_ref[...].astype(jnp.float32)
    base = z * CHIP

    def places(i, carry):
        d = (base + i) & (ND - 1)
        for q in range(NQ):
            place_ref[q, i] = CHIP + i - d + ND * shift_ref[0, q] + ((d + shift_ref[1, q]) & (ND - 1))
        return carry

    lax.fori_loop(0, CHIP, places, 0, unroll=2)

    @pl.when(jnp.logical_or(odd_core, has_above))
    def _():
        pl.semaphore_wait(relay, core + one(has_above))

    each_chunk(send_rest)

    load.wait()

    def advance(ch):
        @pl.when(has_south)
        def _():
            to_north(ch).wait_recv()

        @pl.when(has_north)
        def _():
            to_south(ch).wait_recv()

        def propagate(j, carry):
            i = ch[1] + j
            a = lat_ref[i]
            b = lon_ref[i]
            up = a > 0.0
            west_in = b > 0.0
            a = jnp.abs(a)
            b = jnp.abs(b)
            from_halo = odd == up

            def substep(e, upstream, m):
                west, east = roll_lon(e, edge_west, edge_east, low_sub, high_sub)
                side = jnp.where(west_in, west, east)
                moved = e - a * (e - upstream)
                moved = moved - b * (e - side)
                return moved * m

            e = xv[i]
            halo = jnp.where(up, south[i], north[i])
            halo_mask = jnp.where(up, mask_south[...], mask_north[...]).astype(jnp.float32)
            first = substep(e, other_row(jnp.where(from_halo, halo, e)), mask)
            halo = substep(halo, other_row(halo), halo_mask)
            second = substep(first, other_row(jnp.where(from_halo, halo, first)), mask)
            mine = core == 0
            g[CHIP + core * COMP + i] = jnp.where(mine, second[:2], second[2:])
            other[i] = jnp.where(mine, second[2:], second[:2])
            return carry

        lax.fori_loop(0, ch[2], propagate, 0, unroll=4)

        for h in range(2):

            @pl.when(sends_up(ch))
            def _():
                to_z(0, h, ch).start()

            @pl.when(sends_down(ch))
            def _():
                to_z(1, h, ch).start()

        swap(ch).start()

    each_chunk(advance)

    def arrive(ch):
        swap_in(ch).wait_recv()
        for source_core in range(2):

            @pl.when(comes_up(source_core, ch))
            def _():
                from_z(0, source_core, ch).wait_recv()

            @pl.when(comes_down(source_core, ch))
            def _():
                from_z(1, source_core, ch).wait_recv()

    each_chunk(arrive)

    def source(i):
        e = g[CHIP + i]
        total = jnp.zeros_like(e)
        for q in range(NQ):
            partner = g[place_ref[q, i]]
            total = total + partner * (partner - e)
        return e + (strength_ref[base + i] * e) * total

    for piece in range(PIECES):

        def for_sibling(i, carry):
            res_sib[i] = source((1 - core) * COMP + i)
            return carry

        lax.fori_loop(piece * PART, (piece + 1) * PART, for_sibling, 0, unroll=4)
        give_back(piece).start()

    def for_me(i, carry):
        out_ref[i, pl.ds(2 * core, 2)] = source(core * COMP + i)
        return carry

    lax.fori_loop(0, COMP, for_me, 0, unroll=4)

    def left(ch):
        @pl.when(has_north)
        def _():
            to_north(ch).wait_send()

        @pl.when(has_south)
        def _():
            to_south(ch).wait_send()

        for h in range(2):

            @pl.when(sends_up(ch))
            def _():
                to_z(0, h, ch).wait_send()

            @pl.when(sends_down(ch))
            def _():
                to_z(1, h, ch).wait_send()

        swap(ch).wait_send()

    each_chunk(left)

    @pl.when(has_north)
    def _():
        mask_to_north().wait_send()

    @pl.when(has_south)
    def _():
        mask_to_south().wait_send()

    for piece in range(PIECES):
        give_back(piece).wait_send()
        take_back(piece).wait_recv()


def solution(mesh):
    n_comp, n_lat = mesh.shape["comp"], mesh.shape["lat"]
    block = pltpu.VMEM((COMP, 4, 8, 128), jnp.float32)
    half = pltpu.VMEM((COMP, 2, 8, 128), jnp.float32)
    small = pltpu.VMEM((4, 8, 128), jnp.int32)
    dma = pltpu.SemaphoreType.DMA

    def per_device(spectrum, courant_lat, courant_lon, sea_mask, strength, quad_shift):
        x = spectrum.reshape(COMP, 2, 16, 128).transpose(0, 2, 1, 3).reshape(COMP, 4, 8, 128)
        mask = sea_mask.reshape(2, 16, 128).transpose(1, 0, 2).reshape(4, 8, 128)
        out = pl.pallas_call(
            functools.partial(kernel, n_comp, n_lat),
            out_shape=pltpu.VMEM((COMP, 4, 8, 128), jnp.float32),
            in_specs=[pl.BlockSpec(memory_space=pltpu.HBM)] * 6,
            out_specs=pl.BlockSpec(memory_space=pltpu.VMEM),
            scratch_shapes=[
                pltpu.SMEM((COMP,), jnp.float32),
                pltpu.SMEM((COMP,), jnp.float32),
                pltpu.SMEM((NF * ND,), jnp.float32),
                pltpu.SMEM((2, NQ), jnp.int32),
                pltpu.SMEM((NQ, CHIP), jnp.int32),
                small,
                block,
                block,
                block,
                small,
                small,
                pltpu.VMEM((3 * CHIP, 2, 8, 128), jnp.float32),
                half,
                half,
                dma((5,)),
                dma,
                dma((2, CHUNKS)),
                dma((2, CHUNKS)),
                dma((2,)),
                dma((2,)),
                dma((2, 2, CHUNKS)),
                dma((2, 2, CHUNKS)),
                dma((CHUNKS,)),
                dma((CHUNKS,)),
                dma((PIECES,)),
                dma((PIECES,)),
                pltpu.SemaphoreType.REGULAR,
            ],
            compiler_params=pltpu.CompilerParams(
                collective_id=0, has_side_effects=True, vmem_limit_bytes=VMEM_BYTES
            ),
        )(x, courant_lat, courant_lon, mask, strength, quad_shift.T)
        return out.reshape(COMP, 16, 2, 128).transpose(0, 2, 1, 3).reshape(COMP, 2, 2048)

    return jax.shard_map(
        per_device,
        mesh=mesh,
        in_specs=(P("comp", "lat", None), P("comp"), P("comp"), P("lat", None), P(), P()),
        out_specs=P("comp", "lat", None),
        check_vma=False,
    )
```

```python
import functools

import jax
import jax.numpy as jnp
from jax import lax
from jax.experimental import pallas as pl
from jax.experimental.pallas import tpu as pltpu
from jax.sharding import PartitionSpec as P

NF = 36
ND = 32
NQ = 4
COMP = 72
CHIP = 2 * COMP
EDGE = 4
STEP = 8
MIDDLE = (COMP - 2 * EDGE) // STEP
EARLY = 2
CHUNKS = MIDDLE + 2
PIECES = 6
PART = COMP // PIECES
VMEM_BYTES = 627 * 1024 * 1024 // 10
ROW = 8
HALF_WAY = 4 * ROW
FAR = (ROW + 1, 2 * ROW + 1, 3 * ROW + 1)

MESH = pl.DeviceIdType.MESH


def roll_lon(e, edge_west, edge_east, low_sub, high_sub):
    down = pltpu.roll(e, 2, axis=1)
    down = jnp.where(low_sub, jnp.concatenate([down[3:], down[:3]], axis=0), down)
    west = pltpu.roll(jnp.where(edge_west, down, e), 1, axis=2)
    up = pltpu.roll(e, 6, axis=1)
    up = jnp.where(high_sub, jnp.concatenate([up[1:], up[:1]], axis=0), up)
    east = pltpu.roll(jnp.where(edge_east, up, e), 127, axis=2)
    return west, east


def kernel(
    n_comp,
    n_lat,
    x_ref,
    lat_any,
    lon_any,
    mask_any,
    strength_any,
    shift_any,
    out_ref,
    lat_ref,
    lon_ref,
    strength_ref,
    shift_ref,
    place_ref,
    mask_ref,
    xv,
    south,
    north,
    mask_south,
    mask_north,
    g,
    other,
    res_sib,
    arg_sem,
    load_sem,
    x_send,
    x_recv,
    m_send,
    m_recv,
    z_send,
    z_recv,
    swap_send,
    swap_recv,
    ret_send,
    ret_recv,
    relay,
):
    comp = lax.axis_index("comp")
    lat = lax.axis_index("lat")
    z = comp // 2
    core = comp % 2
    n_z = n_comp // 2
    has_south = lat > 0
    has_north = lat < n_lat - 1
    has_below = z > 0
    has_above = z < n_z - 1
    sib = z * 2 + 1 - core
    odd_core = core == 1

    first_chunk = (0, 0, EDGE)
    last_chunk = (CHUNKS - 1, COMP - EDGE, EDGE)

    def middle_chunk(k):
        return (k + 1, EDGE + STEP * k, STEP)

    def each_chunk(act):
        act(first_chunk)

        def step(k, carry):
            act(middle_chunk(k))
            return carry

        lax.fori_loop(0, MIDDLE, step, 0)
        act(last_chunk)

    def span_at(offset, ch):
        return pl.ds(offset + ch[1], ch[2])

    def rows(ch):
        return span_at(0, ch)

    load = pltpu.make_async_copy(x_ref, xv, load_sem)

    def to_north(ch):
        return pltpu.make_async_remote_copy(
            src_ref=x_ref.at[rows(ch)],
            dst_ref=south.at[rows(ch)],
            send_sem=x_send.at[0, ch[0]],
            recv_sem=x_recv.at[0, ch[0]],
            device_id={"lat": lat + 1},
            device_id_type=MESH,
        )

    def to_south(ch):
        return pltpu.make_async_remote_copy(
            src_ref=x_ref.at[rows(ch)],
            dst_ref=north.at[rows(ch)],
            send_sem=x_send.at[1, ch[0]],
            recv_sem=x_recv.at[1, ch[0]],
            device_id={"lat": lat - 1},
            device_id_type=MESH,
        )

    def mask_to_north():
        return pltpu.make_async_remote_copy(
            src_ref=mask_any,
            dst_ref=mask_south,
            send_sem=m_send.at[0],
            recv_sem=m_recv.at[0],
            device_id={"lat": lat + 1},
            device_id_type=MESH,
        )

    def mask_to_south():
        return pltpu.make_async_remote_copy(
            src_ref=mask_any,
            dst_ref=mask_north,
            send_sem=m_send.at[1],
            recv_sem=m_recv.at[1],
            device_id={"lat": lat - 1},
            device_id_type=MESH,
        )

    def half_src(h, ch):
        if h == 0:
            return g.at[span_at(CHIP + core * COMP, ch)]
        return other.at[rows(ch)]

    def to_z(direction, h, ch):
        third = 0 if direction == 0 else 2
        target = (z + 1 if direction == 0 else z - 1) * 2 + (core if h == 0 else 1 - core)
        return pltpu.make_async_remote_copy(
            src_ref=half_src(h, ch),
            dst_ref=g.at[span_at(third * CHIP + core * COMP, ch)],
            send_sem=z_send.at[direction, h, ch[0]],
            recv_sem=z_recv.at[direction, core, ch[0]],
            device_id={"comp": target},
            device_id_type=MESH,
        )

    def skipped(direction, parity, source_core, ch):
        if direction == 0:
            first = jnp.where(parity == 0, 4, 0)
            last = 12
            owner = 0
        else:
            first = 60
            last = jnp.where(parity == 0, 72, 68)
            owner = 1
        start = ch[1]
        return jnp.logical_and(source_core == owner, jnp.logical_and(start >= first, start < last))

    def sends_up(ch):
        return jnp.logical_and(has_above, jnp.logical_not(skipped(0, z % 2, core, ch)))

    def sends_down(ch):
        return jnp.logical_and(has_below, jnp.logical_not(skipped(1, z % 2, core, ch)))

    def comes_up(source_core, ch):
        return jnp.logical_and(has_below, jnp.logical_not(skipped(0, (z + 1) % 2, source_core, ch)))

    def comes_down(source_core, ch):
        return jnp.logical_and(has_above, jnp.logical_not(skipped(1, (z + 1) % 2, source_core, ch)))

    def from_z(direction, source_core, ch):
        third = 0 if direction == 0 else 2
        here = g.at[span_at(third * CHIP + source_core * COMP, ch)]
        return pltpu.make_async_remote_copy(
            src_ref=here,
            dst_ref=here,
            send_sem=z_send.at[direction, 0, ch[0]],
            recv_sem=z_recv.at[direction, source_core, ch[0]],
            device_id={"comp": sib},
            device_id_type=MESH,
        )

    def swap(ch):
        return pltpu.make_async_remote_copy(
            src_ref=other.at[rows(ch)],
            dst_ref=g.at[span_at(CHIP + core * COMP, ch)],
            send_sem=swap_send.at[ch[0]],
            recv_sem=swap_recv.at[ch[0]],
            device_id={"comp": sib},
            device_id_type=MESH,
        )

    def swap_in(ch):
        here = g.at[span_at(CHIP + (1 - core) * COMP, ch)]
        return pltpu.make_async_remote_copy(
            src_ref=here,
            dst_ref=here,
            send_sem=swap_send.at[ch[0]],
            recv_sem=swap_recv.at[ch[0]],
            device_id={"comp": sib},
            device_id_type=MESH,
        )

    def give_back(piece):
        span = pl.ds(piece * PART, PART)
        return pltpu.make_async_remote_copy(
            src_ref=res_sib.at[span],
            dst_ref=out_ref.at[span, pl.ds(2 * core, 2)],
            send_sem=ret_send.at[piece],
            recv_sem=ret_recv.at[piece],
            device_id={"comp": sib},
            device_id_type=MESH,
        )

    def take_back(piece):
        span = pl.ds(piece * PART, PART)
        return pltpu.make_async_remote_copy(
            src_ref=res_sib.at[span],
            dst_ref=out_ref.at[span, pl.ds(2 * (1 - core), 2)],
            send_sem=ret_send.at[piece],
            recv_sem=ret_recv.at[piece],
            device_id={"comp": sib},
            device_id_type=MESH,
        )

    fetches = [
        pltpu.make_async_copy(source_ref, target_ref, arg_sem.at[place])
        for place, (source_ref, target_ref) in enumerate(
            (
                (lat_any, lat_ref),
                (lon_any, lon_ref),
                (mask_any, mask_ref),
                (strength_any, strength_ref),
                (shift_any, shift_ref),
            )
        )
    ]

    barrier = pltpu.get_barrier_semaphore()

    def greet(**where):
        pl.semaphore_signal(barrier, inc=1, device_id=where, device_id_type=MESH)

    @pl.when(odd_core)
    def _():
        greet(comp=sib)

    @pl.when(has_below)
    def _():
        greet(comp=2 * z - 2)

    @pl.when(has_south)
    def _():
        greet(lat=lat - 1)

    @pl.when(has_north)
    def _():
        greet(lat=lat + 1)

    for far in FAR:

        @pl.when(jnp.logical_and(jnp.logical_and(core == 0, lat % ROW == 0), jnp.logical_and(lat >= far, lat <= HALF_WAY)))
        def _():
            greet(lat=lat - far)

    for fetch in fetches:
        fetch.start()
    load.start()

    @pl.when(jnp.logical_not(has_south))
    def _():
        south[...] = jnp.zeros_like(south)
        mask_south[...] = jnp.zeros_like(mask_south)

    @pl.when(jnp.logical_not(has_north))
    def _():
        north[...] = jnp.zeros_like(north)
        mask_north[...] = jnp.zeros_like(mask_north)

    @pl.when(jnp.logical_not(has_below))
    def _():
        g[pl.ds(0, CHIP)] = jnp.zeros((CHIP, 2, 8, 128), jnp.float32)

    @pl.when(jnp.logical_not(has_above))
    def _():
        g[pl.ds(2 * CHIP, CHIP)] = jnp.zeros((CHIP, 2, 8, 128), jnp.float32)

    def one(flag):
        return flag.astype(jnp.int32)

    ahead = sum(one(lat + far <= HALF_WAY) for far in FAR) * one(lat % ROW == ROW - 1)
    held_back = jnp.logical_and(odd_core, ahead > 0)
    line = one(has_south) + one(has_north)
    pl.semaphore_wait(barrier, line + (1 - core) * (ahead + 1 + 2 * one(has_above)))

    def tell(target):
        pl.semaphore_signal(relay, inc=1, device_id={"comp": target}, device_id_type=MESH)

    @pl.when(core == 0)
    def _():
        tell(2 * z + 1)

        @pl.when(has_above)
        def _():
            tell(2 * z + 2)
            tell(2 * z + 3)

    @pl.when(has_north)
    def _():
        mask_to_north().start()

    @pl.when(has_south)
    def _():
        mask_to_south().start()

    def send_rows(ch):
        @pl.when(jnp.logical_and(has_north, jnp.logical_or(jnp.logical_not(held_back), ch[0] <= EARLY)))
        def _():
            to_north(ch).start()

        @pl.when(has_south)
        def _():
            to_south(ch).start()

    def send_rest(ch):
        @pl.when(jnp.logical_and(held_back, ch[0] > EARLY))
        def _():
            to_north(ch).start()

    each_chunk(send_rows)

    @pl.when(has_south)
    def _():
        mask_to_north().wait_recv()

    @pl.when(has_north)
    def _():
        mask_to_south().wait_recv()

    shape = (4, 8, 128)
    lane = lax.broadcasted_iota(jnp.int32, shape, 2)
    sub = lax.broadcasted_iota(jnp.int32, shape, 1)
    edge_west = lane == 127
    edge_east = lane == 0
    low_sub = sub < 2
    high_sub = sub >= 6
    odd = (sub & 1) == 1

    def other_row(e):
        return jnp.where(odd, pltpu.roll(e, 1, axis=1), pltpu.roll(e, 7, axis=1))

    for fetch in fetches:
        fetch.wait()
    mask = mask_ref[...].astype(jnp.float32)
    base = z * CHIP

    def places(i, carry):
        d = (base + i) & (ND - 1)
        for q in range(NQ):
            place_ref[q, i] = CHIP + i - d + ND * shift_ref[0, q] + ((d + shift_ref[1, q]) & (ND - 1))
        return carry

    lax.fori_loop(0, CHIP, places, 0, unroll=2)

    @pl.when(jnp.logical_or(odd_core, has_below))
    def _():
        pl.semaphore_wait(relay, core + one(has_below))

    each_chunk(send_rest)

    load.wait()

    def advance(ch):
        @pl.when(has_south)
        def _():
            to_north(ch).wait_recv()

        @pl.when(has_north)
        def _():
            to_south(ch).wait_recv()

        def propagate(j, carry):
            i = ch[1] + j
            a = lat_ref[i]
            b = lon_ref[i]
            up = a > 0.0
            west_in = b > 0.0
            a = jnp.abs(a)
            b = jnp.abs(b)
            from_halo = odd == up

            def substep(e, upstream, m):
                west, east = roll_lon(e, edge_west, edge_east, low_sub, high_sub)
                side = jnp.where(west_in, west, east)
                moved = e - a * (e - upstream)
                moved = moved - b * (e - side)
                return moved * m

            e = xv[i]
            halo = jnp.where(up, south[i], north[i])
            halo_mask = jnp.where(up, mask_south[...], mask_north[...]).astype(jnp.float32)
            first = substep(e, other_row(jnp.where(from_halo, halo, e)), mask)
            halo = substep(halo, other_row(halo), halo_mask)
            second = substep(first, other_row(jnp.where(from_halo, halo, first)), mask)
            mine = core == 0
            g[CHIP + core * COMP + i] = jnp.where(mine, second[:2], second[2:])
            other[i] = jnp.where(mine, second[2:], second[:2])
            return carry

        lax.fori_loop(0, ch[2], propagate, 0, unroll=4)

        swap(ch).start()

        for h in range(2):

            @pl.when(sends_up(ch))
            def _():
                to_z(0, h, ch).start()

            @pl.when(sends_down(ch))
            def _():
                to_z(1, h, ch).start()


    each_chunk(advance)

    def arrive(ch):
        swap_in(ch).wait_recv()
        for source_core in range(2):

            @pl.when(comes_up(source_core, ch))
            def _():
                from_z(0, source_core, ch).wait_recv()

            @pl.when(comes_down(source_core, ch))
            def _():
                from_z(1, source_core, ch).wait_recv()

    each_chunk(arrive)

    def source(i):
        e = g[CHIP + i]
        total = jnp.zeros_like(e)
        for q in range(NQ):
            partner = g[place_ref[q, i]]
            total = total + partner * (partner - e)
        return e + (strength_ref[base + i] * e) * total

    for piece in range(PIECES):

        def for_sibling(i, carry):
            res_sib[i] = source((1 - core) * COMP + i)
            return carry

        lax.fori_loop(piece * PART, (piece + 1) * PART, for_sibling, 0, unroll=4)
        give_back(piece).start()

    def for_me(i, carry):
        out_ref[i, pl.ds(2 * core, 2)] = source(core * COMP + i)
        return carry

    lax.fori_loop(0, COMP, for_me, 0, unroll=4)

    def left(ch):
        @pl.when(has_north)
        def _():
            to_north(ch).wait_send()

        @pl.when(has_south)
        def _():
            to_south(ch).wait_send()

        for h in range(2):

            @pl.when(sends_up(ch))
            def _():
                to_z(0, h, ch).wait_send()

            @pl.when(sends_down(ch))
            def _():
                to_z(1, h, ch).wait_send()

        swap(ch).wait_send()

    each_chunk(left)

    @pl.when(has_north)
    def _():
        mask_to_north().wait_send()

    @pl.when(has_south)
    def _():
        mask_to_south().wait_send()

    for piece in range(PIECES):
        give_back(piece).wait_send()
        take_back(piece).wait_recv()


def solution(mesh):
    n_comp, n_lat = mesh.shape["comp"], mesh.shape["lat"]
    block = pltpu.VMEM((COMP, 4, 8, 128), jnp.float32)
    half = pltpu.VMEM((COMP, 2, 8, 128), jnp.float32)
    small = pltpu.VMEM((4, 8, 128), jnp.int32)
    dma = pltpu.SemaphoreType.DMA

    def per_device(spectrum, courant_lat, courant_lon, sea_mask, strength, quad_shift):
        x = spectrum.reshape(COMP, 2, 16, 128).transpose(0, 2, 1, 3).reshape(COMP, 4, 8, 128)
        mask = sea_mask.reshape(2, 16, 128).transpose(1, 0, 2).reshape(4, 8, 128)
        out = pl.pallas_call(
            functools.partial(kernel, n_comp, n_lat),
            out_shape=pltpu.VMEM((COMP, 4, 8, 128), jnp.float32),
            in_specs=[pl.BlockSpec(memory_space=pltpu.HBM)] * 6,
            out_specs=pl.BlockSpec(memory_space=pltpu.VMEM),
            scratch_shapes=[
                pltpu.SMEM((COMP,), jnp.float32),
                pltpu.SMEM((COMP,), jnp.float32),
                pltpu.SMEM((NF * ND,), jnp.float32),
                pltpu.SMEM((2, NQ), jnp.int32),
                pltpu.SMEM((NQ, CHIP), jnp.int32),
                small,
                block,
                block,
                block,
                small,
                small,
                pltpu.VMEM((3 * CHIP, 2, 8, 128), jnp.float32),
                half,
                half,
                dma((5,)),
                dma,
                dma((2, CHUNKS)),
                dma((2, CHUNKS)),
                dma((2,)),
                dma((2,)),
                dma((2, 2, CHUNKS)),
                dma((2, 2, CHUNKS)),
                dma((CHUNKS,)),
                dma((CHUNKS,)),
                dma((PIECES,)),
                dma((PIECES,)),
                pltpu.SemaphoreType.REGULAR,
            ],
            compiler_params=pltpu.CompilerParams(
                collective_id=0, has_side_effects=True, vmem_limit_bytes=VMEM_BYTES
            ),
        )(x, courant_lat, courant_lon, mask, strength, quad_shift.T)
        return out.reshape(COMP, 16, 2, 128).transpose(0, 2, 1, 3).reshape(COMP, 2, 2048)

    return jax.shard_map(
        per_device,
        mesh=mesh,
        in_specs=(P("comp", "lat", None), P("comp"), P("comp"), P("lat", None), P(), P()),
        out_specs=P("comp", "lat", None),
        check_vma=False,
    )
```
